32 devices in a mesh: groups: 2 (over x), tensor: 16 (over z, y, core).
Axes of the slice: x: 2, y: 2, z: 4, core: 2. Of those that a mesh axis runs over, the one named last changes fastest.
Arguments:
- activations: bfloat16 [2048, 8192], P('groups', 'tensor'), parts along dimension 0, may hold values from -6 to 6
- gate_pre: bfloat16 [2048, 28672], P('groups', 'tensor'), parts along dimension 0, may hold values from -6 to 6
- up_pre: bfloat16 [2048, 28672], P('groups', 'tensor'), parts along dimension 0, may hold values from -6 to 6
- out_grad: bfloat16 [2048, 8192], P('groups', 'tensor'), parts along dimension 0, may hold values from -6 to 6
- down_weight: bfloat16 [28672, 8192], P('tensor'), may hold values from -0.0625 to 0.0625
- in_proj_down: bfloat16 [64, 28672], P(None, 'tensor'), may hold values from -0.03125 to 0.03125
- out_proj_down: bfloat16 [64, 8192], replicated, may hold values from -0.0625 to 0.0625
- in_proj_up: bfloat16 [64, 8192], P(None, 'tensor'), may hold values from -0.0625 to 0.0625
- out_proj_up: bfloat16 [64, 28672], P(None, 'tensor'), may hold values from -0.03125 to 0.03125
- segments: int32 [2048], P('groups'), parts along dimension 0, may hold values from 0 to 15, never falling along the last dimension, each value on 1 to 128 neighbouring positions
- labels: int32 [32], P('groups'), parts along dimension 0, may hold values from 0 to 1, as said below
- queries: bfloat16 [1024, 8192], P('tensor'), may hold values from -0.005859375 to 0.005859375
Outputs:
- scores: float32 [16, 1024], P('groups', 'tensor'), parts along dimension 0
The draws below stay inside these ranges and needn't reach their ends.
There are 2 independent parts, one for each index of `groups`. The reference program is written for one: setup_inputs(seed, part) draws one part's arguments, and reference() takes and returns one part's arrays. A program takes and returns all parts, laid end to end along the dimension named above; an argument that names none is the same for every part. Nothing has to cross between parts.
Inputs may be any that keep to these rules, and one draw needn't show every extreme that they name: labels[2k] + labels[2k + 1] == 1 for every pair k.
All inputs are finite; a program needn't handle non-finite values.
Results may differ from the reference program's by a relative error of at most 0.0041.
Values may be sent and summed in bfloat16 or wider, within the bound.
No kernel may reach another device: no remote copies, remote signals or barrier semaphores. Data moves between devices by JAX's collectives and lax.ppermute only.
A program may use at most 128 MiB of HBM per device.

```python
import math
import jax
import jax.numpy as jnp
import numpy as np
from jax import lax

D = 8192
FF = 28672
KI = 64
KO = 64
TOK = 1024
PAIR_TOK = 128
PAIRS = 8
SEQS = 16
QUERIES = 1024


def draw_labels(key, part):
    key = jax.random.fold_in(key, 7)
    first = jax.random.randint(key, (PAIRS,), 0, 2)
    return jnp.stack([first, 1 - first], axis=1).reshape(SEQS).astype(jnp.int32)


def shard_levels(own_key, shape, shards, smallest, largest):
    gain, own = 1.0, jax.random.fold_in(own_key, 6)
    for dim, parts in shards:
        steps = jnp.exp(jax.random.uniform(jax.random.fold_in(own, dim), (parts,), jnp.float32, smallest / len(shards), largest / len(shards)))
        gain = gain * jnp.repeat(steps, shape[dim] // parts).reshape([-1 if axis == dim else 1 for axis in range(len(shape))])
    return gain


def split_up(amount, total, reach, lean):
    loads = [(1 << 20) // math.isqrt(standing ** lean) + 1 for standing in range(2, amount + 1)]
    spare, counts = total - reach - (amount - 1), [1] * (amount - 1)
    while spare > 0:
        candidates = [i for i in range(amount - 1) if counts[i] < reach]
        pool, budget = sum([loads[i] for i in candidates]), spare
        for i in candidates:
            more = min(reach - counts[i], max(1, budget * loads[i] // pool), spare)
            counts[i] = counts[i] + more
            spare = spare - more
    return np.array([reach] + counts)


def ragged(stream_key, count, total, limit, slope):
    if count == 2:
        one = jax.random.randint(stream_key, (), max(1, total - limit), min(limit, total - 1) + 1)
        return jnp.stack([one, total - one])
    lengths = jnp.asarray(split_up(count, total, limit, slope), jnp.int32)
    couples = (count - 1) // 2
    giver, taker = lengths[1:1 + 2 * couples:2], lengths[2:2 + 2 * couples:2]
    room = jnp.minimum(giver - 1, limit - taker)
    passed = jax.random.randint(jax.random.fold_in(stream_key, 1), (couples,), 0, 1 << 20) % (room + 1)
    lengths = lengths.at[1:1 + 2 * couples:2].set(giver - passed).at[2:2 + 2 * couples:2].set(taker + passed)
    return lengths[jax.random.permutation(jax.random.fold_in(stream_key, 2), count)]


def scatter_about(key, extent, scale, limit, split=(), kind=jnp.bfloat16):
    level = shard_levels(key, extent, split, -0.22, 0.18) if split else 1.0
    values = jax.random.normal(key, extent, jnp.float32) * scale * level
    return jnp.minimum(jnp.maximum(values, -limit), limit).astype(kind)


def setup_inputs(seed: int = 0, part: int = 0) -> dict:
    arg_keys = jax.random.split(jax.random.key(seed), 13)
    part_keys = jax.random.split(jax.random.fold_in(arg_keys[12], part), 13)
    activations = scatter_about(part_keys[0], (TOK, D), 1.0, 6.0, ((1, 16),))
    gate_pre = scatter_about(part_keys[1], (TOK, FF), 1.0, 6.0, ((1, 16),))
    up_pre = scatter_about(part_keys[2], (TOK, FF), 1.0, 6.0, ((1, 16),))
    out_grad = scatter_about(part_keys[3], (TOK, D), 1.0, 6.0, ((1, 16),))
    down_weight = scatter_about(arg_keys[4], (FF, D), D ** -0.5, 0.0625, ((0, 16),))
    in_proj_down = scatter_about(arg_keys[5], (KI, FF), FF ** -0.5, 0.03125, ((1, 16),))
    out_proj_down = scatter_about(arg_keys[6], (KO, D), D ** -0.5, 0.0625)
    in_proj_up = scatter_about(arg_keys[7], (KI, D), D ** -0.5, 0.0625, ((1, 16),))
    out_proj_up = scatter_about(arg_keys[8], (KO, FF), FF ** -0.5, 0.03125, ((1, 16),))
    segments = jnp.searchsorted(jnp.cumsum(ragged(part_keys[9], SEQS, TOK, PAIR_TOK, 2)), jnp.arange(TOK), side="right").astype(jnp.int32)
    labels = draw_labels(jax.random.fold_in(jax.random.fold_in(arg_keys[12], part), 71), part)
    queries = scatter_about(arg_keys[11], (QUERIES, 2 * KO * KI), (2 * KO * KI * PAIR_TOK) ** -0.5, 0.005859375, ((0, 16),))
    return dict(activations=activations, gate_pre=gate_pre, up_pre=up_pre, out_grad=out_grad, down_weight=down_weight, in_proj_down=in_proj_down, out_proj_down=out_proj_down, in_proj_up=in_proj_up, out_proj_up=out_proj_up, segments=segments, labels=labels, queries=queries)


def pair_outer(weight, left, right):
    return jnp.einsum("tp,tk,tj->pkj", weight, left, right, precision=lax.Precision.HIGHEST).reshape(weight.shape[1], -1)


def reference(activations, gate_pre, up_pre, out_grad, down_weight, in_proj_down, out_proj_down, in_proj_up, out_proj_up, segments, labels, queries):
    silu_gate = jax.nn.silu(gate_pre.astype(jnp.float32))
    hidden = (silu_gate * up_pre.astype(jnp.float32)).astype(jnp.bfloat16)
    dgrad = jnp.dot(out_grad, down_weight.T, preferred_element_type=jnp.float32)
    up_grad = (dgrad * silu_gate).astype(jnp.bfloat16)
    a_down = jnp.dot(hidden, in_proj_down.T, preferred_element_type=jnp.float32)
    b_down = jnp.dot(out_grad, out_proj_down.T, preferred_element_type=jnp.float32)
    a_up = jnp.dot(activations, in_proj_up.T, preferred_element_type=jnp.float32)
    b_up = jnp.dot(up_grad, out_proj_up.T, preferred_element_type=jnp.float32)
    signs = (2 * labels[segments] - 1).astype(jnp.float32)
    pair_of = segments // 2
    weight = jnp.where(pair_of[:, None] == jnp.arange(PAIRS, dtype=jnp.int32)[None, :], signs[:, None], jnp.float32(0.0))
    grads = jnp.concatenate([pair_outer(weight, b_down, a_down), pair_outer(weight, b_up, a_up)], axis=1).astype(jnp.bfloat16)
    return jnp.dot(grads, queries.T, preferred_element_type=jnp.float32)
```

```python
import functools

import jax
import jax.numpy as jnp
import numpy as np
from jax import lax
from jax.experimental import pallas as pl
from jax.experimental.pallas import tpu as pltpu
from jax.sharding import PartitionSpec as P

F32, BF16 = jnp.float32, jnp.bfloat16
VMEM_LIMIT = 40 * 1024 * 1024


def dot_t(left, right, precision=None):
    return lax.dot_general(
        left, right, (((1,), (1,)), ((), ())), preferred_element_type=F32, precision=precision
    )


def ring_of(chips):
    if chips == 8:
        return [0, 2, 4, 6, 7, 5, 3, 1]
    return list(range(chips))


def step_kernel(blocks, src_ref, *refs):
    lefts, weights = refs[:blocks], refs[blocks : 2 * blocks]
    acc_ref = refs[2 * blocks] if len(refs) == 2 * blocks + 2 else None
    out_ref = refs[-1]
    total = None if acc_ref is None else acc_ref[...]
    for left, weight in zip(lefts, weights):
        part = dot_t(left[...], weight[...])
        total = part if total is None else total + part
    out_ref[...] = total


def tile_of(units):
    return 256 if units % 256 == 0 else units


def add_step(src, offset, lefts, weight, acc):
    tokens, depth = lefts[0].shape
    units = weight.shape[0]
    tile, blocks = tile_of(units), len(lefts)
    whole = pl.BlockSpec((tokens, depth), lambda i, s: (0, 0))
    tiles = pl.BlockSpec((tokens, tile), lambda i, s: (0, i))
    columns = [
        pl.BlockSpec((tile, depth), lambda i, s, m=m: (i, s[offset + m])) for m in range(blocks)
    ]
    ins = [*lefts, *([weight] * blocks)]
    specs = [whole] * blocks + columns
    aliases = {}
    if acc is not None:
        ins.append(acc)
        specs.append(tiles)
        aliases = {len(ins): 0}
    return pl.pallas_call(
        functools.partial(step_kernel, blocks),
        grid_spec=pltpu.PrefetchScalarGridSpec(
            num_scalar_prefetch=1, grid=(units // tile,), in_specs=specs, out_specs=tiles
        ),
        out_shape=jax.ShapeDtypeStruct((tokens, units), F32),
        input_output_aliases=aliases,
        cost_estimate=pl.CostEstimate(
            flops=2 * tokens * units * depth * blocks,
            bytes_accessed=units * tokens * 8 + units * depth * blocks * 2,
            transcendentals=0,
        ),
        compiler_params=pltpu.CompilerParams(vmem_limit_bytes=VMEM_LIMIT),
    )(src, *ins)


def pair_sums(weight, b, a, out_ref):
    kos, pairs = b.shape[0], weight.shape[0]
    kis = a.shape[0]
    left = jnp.concatenate([weight * b[k : k + 1, :] for k in range(kos)], axis=0)
    sums = dot_t(left, a, lax.Precision.HIGHEST)
    half = kos // 2
    for r in range(half):
        low = sums[r * pairs : (r + 1) * pairs]
        high = sums[(r + half) * pairs : (r + half + 1) * pairs]
        out_ref[:, r * 2 * kis : (r + 1) * 2 * kis] = jnp.concatenate([low, high], axis=1)


def pair_kernel(weight_ref, b_ref, a_ref, out_ref):
    pair_sums(weight_ref[...], b_ref[...], a_ref[...], out_ref)


def pair_outer(weight, b, a):
    return pl.pallas_call(
        pair_kernel,
        out_shape=jax.ShapeDtypeStruct((weight.shape[0], b.shape[0] * a.shape[0]), F32),
        compiler_params=pltpu.CompilerParams(vmem_limit_bytes=VMEM_LIMIT),
    )(weight, b, a)


def last_kernel(
    src_ref, f0, f1, b0, b1, w0, w1, acc_ref, silu_ref, proj_ref, weight_ref, a_ref, out_ref, b_acc
):
    step = pl.program_id(0)
    half = f0.shape[0]

    @pl.when(step == 0)
    def _():
        b_acc[...] = jnp.zeros_like(b_acc)

    for row, own, other in ((0, f0, f1), (half, b0, b1)):
        rows = slice(row, row + half)
        grad = acc_ref[rows, :] + dot_t(own[...], w0[...]) + dot_t(other[...], w1[...])
        up = (grad * silu_ref[rows, :]).astype(BF16)
        b_acc[:, rows] += dot_t(proj_ref[...], up)

    @pl.when(step == pl.num_programs(0) - 1)
    def _():
        pair_sums(weight_ref[...], b_acc[...], a_ref[...], out_ref)


def last_step(src, offset, halves, weight, acc, silu, proj, pair_weight, a_up):
    half, depth = halves[0].shape
    tokens, units = acc.shape
    kos, kis, pairs = proj.shape[0], a_up.shape[0], pair_weight.shape[0]
    tile = tile_of(units)
    piece = pl.BlockSpec((half, depth), lambda i, s: (0, 0))
    tiles = pl.BlockSpec((tokens, tile), lambda i, s: (0, i))
    columns = [pl.BlockSpec((tile, depth), lambda i, s, m=m: (i, s[offset + m])) for m in range(2)]
    return pl.pallas_call(
        last_kernel,
        grid_spec=pltpu.PrefetchScalarGridSpec(
            num_scalar_prefetch=1,
            grid=(units // tile,),
            in_specs=[piece] * 4
            + columns
            + [
                tiles,
                tiles,
                pl.BlockSpec((kos, tile), lambda i, s: (0, i)),
                pl.BlockSpec((pairs, tokens), lambda i, s: (0, 0)),
                pl.BlockSpec((kis, tokens), lambda i, s: (0, 0)),
            ],
            out_specs=pl.BlockSpec((pairs, kos * kis), lambda i, s: (0, 0)),
            scratch_shapes=[pltpu.VMEM((kos, tokens), F32)],
        ),
        out_shape=jax.ShapeDtypeStruct((pairs, kos * kis), F32),
        cost_estimate=pl.CostEstimate(
            flops=2 * tokens * units * (2 * depth + kos),
            bytes_accessed=units * tokens * 8 + units * depth * 4,
            transcendentals=0,
        ),
        compiler_params=pltpu.CompilerParams(vmem_limit_bytes=VMEM_LIMIT),
    )(src, *halves, weight, weight, acc, silu, proj, pair_weight, a_up)


def swap(value, bit, devices):
    return lax.ppermute(value, "tensor", [(i, i ^ bit) for i in range(devices)])


def halves_of(value, mine, axis):
    half = value.shape[axis] // 2
    low, high = lax.slice_in_dim(value, 0, half, axis=axis), lax.slice_in_dim(value, half, 2 * half, axis=axis)
    return jnp.where(mine == 0, low, high), jnp.where(mine == 0, high, low)


def all_sum(value, me, devices, splits, axis):
    bits = [1 << i for i in range(devices.bit_length() - 1)]
    for bit in bits[:splits]:
        keep, give = halves_of(value, (me // bit) % 2, axis)
        value = keep + swap(give, bit, devices)
    for bit in bits[splits:]:
        value = value + swap(value, bit, devices)
    for bit in reversed(bits[:splits]):
        other = swap(value, bit, devices)
        mine = (me // bit) % 2
        value = jnp.where(
            mine == 0,
            jnp.concatenate([value, other], axis=axis),
            jnp.concatenate([other, value], axis=axis),
        )
    return value


def per_device(
    devices,
    activations,
    gate_pre,
    up_pre,
    out_grad,
    down_weight,
    in_proj_down,
    out_proj_down,
    in_proj_up,
    out_proj_up,
    segments,
    labels,
    queries,
):
    tokens, depth = out_grad.shape
    me = lax.axis_index("tensor")
    chips = devices // 2
    ring = ring_of(chips)
    far = chips // 2
    place = {chip: i for i, chip in enumerate(ring)}

    table = np.zeros((devices, devices), np.int32)
    for device in range(devices):
        chip, core = divmod(device, 2)
        order = [chip]
        for step in range(1, far):
            order += [ring[(place[chip] - step) % chips], ring[(place[chip] + step) % chips]]
        order.append(ring[(place[chip] + far) % chips])
        table[device] = [2 * c + k for c in order for k in (core, 1 - core)]
    src = lax.dynamic_index_in_dim(jnp.asarray(table), me, 0, keepdims=False)

    ahead = [
        (2 * ring[i] + core, 2 * ring[(i + 1) % chips] + core) for i in range(chips) for core in (0, 1)
    ]
    back = [(b, a) for a, b in ahead]

    steps = [[out_grad]]
    f = b = out_grad
    for _ in range(1, far):
        f = lax.ppermute(f, "tensor", ahead)
        b = lax.ppermute(b, "tensor", back)
        steps.append([f, b])
    f_last = lax.ppermute(f[: tokens // 2], "tensor", ahead)
    b_last = lax.ppermute(b[tokens // 2 :], "tensor", back)

    silu_gate = jax.nn.silu(gate_pre.astype(F32))
    hidden = (silu_gate * up_pre.astype(F32)).astype(BF16)
    a_down = dot_t(in_proj_down, hidden)
    own_columns = lax.dynamic_slice_in_dim(out_proj_down, me * depth, depth, axis=1)
    a_up = dot_t(in_proj_up, activations)
    b_down = dot_t(own_columns, out_grad)
    both = all_sum(jnp.concatenate([a_up, b_down], axis=0), me, devices, 4, 0)
    kis = a_up.shape[0]
    a_up, b_down = both[:kis], both[kis:]

    seq_count = labels.shape[0]
    seqs = jnp.arange(seq_count, dtype=jnp.int32)[:, None]
    signs = (2 * labels - 1).astype(F32)
    per_seq = jnp.where(segments[None, :] == seqs, signs[:, None], F32(0.0))
    pair_weight = per_seq.reshape(seq_count // 2, 2, tokens).sum(axis=1)

    kos = b_down.shape[0]
    asked = queries.shape[0]
    q = queries.reshape(asked, 2, 2, kos // 2, kis).transpose(1, 0, 3, 2, 4).reshape(2, asked, kos * kis)
    g_down = all_sum(pair_outer(pair_weight, b_down, a_down), me, devices, 1, 1)
    s_down = dot_t(g_down.astype(BF16), q[0])

    acc = None
    offset = 0
    for blocks in steps:
        lefts = [x for block in blocks for x in (block, swap(block, 1, devices))]
        acc = add_step(src, offset, lefts, down_weight, acc)
        offset += len(lefts)
    halves = [f_last, swap(f_last, 1, devices), b_last, swap(b_last, 1, devices)]
    g_up = last_step(
        src, offset, halves, down_weight, acc, silu_gate, out_proj_up, pair_weight, a_up
    )
    g_up = all_sum(g_up, me, devices, 1, 1)
    return s_down + dot_t(g_up.astype(BF16), q[1])


def solution(mesh):
    in_specs = (
        P("groups", "tensor"),
        P("groups", "tensor"),
        P("groups", "tensor"),
        P("groups", "tensor"),
        P("tensor", None),
        P(None, "tensor"),
        P(),
        P(None, "tensor"),
        P(None, "tensor"),
        P("groups"),
        P("groups"),
        P("tensor", None),
    )
    return jax.shard_map(
        functools.partial(per_device, mesh.shape["tensor"]),
        mesh=mesh,
        in_specs=in_specs,
        out_specs=P("groups", "tensor"),
        check_vma=False,
    )
```

```python
import functools

import jax
import jax.numpy as jnp
import numpy as np
from jax import lax
from jax.experimental import pallas as pl
from jax.experimental.pallas import tpu as pltpu
from jax.sharding import PartitionSpec as P

F32, BF16 = jnp.float32, jnp.bfloat16
VMEM_LIMIT = 30 * 1024 * 1024
SMALL = pl.CostEstimate(flops=1000, bytes_accessed=1000, transcendentals=0)


def dot_t(left, right, precision=None):
    return lax.dot_general(
        left, right, (((1,), (1,)), ((), ())), preferred_element_type=F32, precision=precision
    )


def ring_of(chips):
    if chips == 8:
        return [0, 2, 4, 6, 7, 5, 3, 1]
    return list(range(chips))


def tile_of(units):
    return 256 if units % 256 == 0 else units


def products(lefts, columns, which):
    total = None
    for left, m in zip(lefts, which):
        part = dot_t(left[...], columns[m][...])
        total = part if total is None else total + part
    return total


def step_kernel(which, src_ref, *refs):
    blocks, owners = len(which[0]), 1 + max(map(max, which))
    lefts, weights = refs[: 2 * blocks], refs[2 * blocks : 2 * blocks + owners]
    before_ref = refs[-2] if len(refs) == 2 * blocks + owners + 2 else None
    out_ref = refs[-1]
    half = out_ref.shape[0] // 2
    for i in range(2):
        rows = slice(i * half, (i + 1) * half)
        total = products(lefts[i * blocks : (i + 1) * blocks], weights, which[i])
        out_ref[rows, :] = total if before_ref is None else total + before_ref[rows, :]


def b_step_kernel(which, src_ref, *refs):
    blocks, owners = len(which[0]), 1 + max(map(max, which))
    lefts, weights = refs[: 2 * blocks], refs[2 * blocks : 2 * blocks + owners]
    acc_ref, silu_ref, proj_ref, out_ref, ups = refs[2 * blocks + owners :]
    step, tile = pl.program_id(0), acc_ref.shape[1]
    half = acc_ref.shape[0] // 2
    for i in range(2):
        rows = slice(i * half, (i + 1) * half)
        total = products(lefts[i * blocks : (i + 1) * blocks], weights, which[i])
        ups[step, rows, :] = ((total + acc_ref[rows, :]) * silu_ref[rows, :]).astype(BF16)

    @pl.when(step == ups.shape[0] - 1)
    def _():
        out_ref[...] = projected(ups, proj_ref)


def projected(ups, proj_ref):
    total, tile = None, ups.shape[2]
    for i in range(ups.shape[0]):
        part = dot_t(ups[i], proj_ref[:, i * tile : (i + 1) * tile])
        total = part if total is None else total + part
    return total


def in_hbm(x):
    return pltpu.with_memory_space_constraint(x, pltpu.HBM)


def in_vmem(x):
    return pltpu.with_memory_space_constraint(x, pltpu.VMEM)


def step_parts(units, half, weight):
    depth = units[0][0][0].shape[1]
    tile = tile_of(weight.shape[0])
    places = sorted({place for unit in units for _, _, place in unit})
    ins, specs, which = [], [], []
    for i in range(2):
        for array, row, _ in (unit[i] for unit in units):
            ins.append(in_hbm(array))
            specs.append(pl.BlockSpec((half, depth), lambda i, s, r=row: (r, 0)))
        which.append([places.index(unit[i][2]) for unit in units])
    ins += [in_hbm(weight)] * len(places)
    specs += [pl.BlockSpec((tile, depth), lambda i, s, m=m: (i, s[m])) for m in places]
    return ins, specs, which, tile


def add_step(src, half, units, weight, before):
    ins, specs, which, tile = step_parts(units, half, weight)
    hidden, tokens = weight.shape[0], 2 * half
    tiles = pl.BlockSpec((tokens, tile), lambda i, s: (0, i))
    aliases = {}
    if before is not None:
        ins.append(in_hbm(before))
        specs.append(tiles)
        aliases = {len(ins): 0}
    return pl.pallas_call(
        functools.partial(step_kernel, which),
        grid_spec=pltpu.PrefetchScalarGridSpec(
            num_scalar_prefetch=1, grid=(hidden // tile,), in_specs=specs, out_specs=tiles
        ),
        out_shape=pltpu.HBM((tokens, hidden), F32),
        input_output_aliases=aliases,
        cost_estimate=SMALL,
        compiler_params=pltpu.CompilerParams(vmem_limit_bytes=VMEM_LIMIT),
    )(src, *ins)


def b_step(src, half, units, weight, before, silu, proj_up):
    ins, specs, which, tile = step_parts(units, half, weight)
    hidden, tokens, kos = weight.shape[0], 2 * half, proj_up.shape[0]
    tiles = pl.BlockSpec((tokens, tile), lambda i, s: (0, i))
    return pl.pallas_call(
        functools.partial(b_step_kernel, which),
        grid_spec=pltpu.PrefetchScalarGridSpec(
            num_scalar_prefetch=1,
            grid=(hidden // tile,),
            in_specs=specs + [tiles, tiles, pl.BlockSpec((kos, hidden), lambda i, s: (0, 0))],
            out_specs=pl.BlockSpec((tokens, kos), lambda i, s: (0, 0)),
            scratch_shapes=[pltpu.VMEM((hidden // tile, tokens, tile), BF16)],
        ),
        out_shape=pltpu.VMEM((tokens, kos), F32),
        cost_estimate=SMALL,
        compiler_params=pltpu.CompilerParams(vmem_limit_bytes=VMEM_LIMIT),
    )(src, *ins, in_hbm(before), in_hbm(silu), proj_up)


def columns_kernel(first, src_ref, weight_ref, out_ref, sems):
    depth = out_ref.shape[2]
    copies = []
    for m in range(2):
        start = pl.multiple_of(src_ref[first + m] * depth, depth)
        copies.append(
            pltpu.make_async_copy(weight_ref.at[:, pl.ds(start, depth)], out_ref.at[m], sems.at[m])
        )
    for copy in copies:
        copy.start()
    for copy in copies:
        copy.wait()


def last_columns(src, weight, depth):
    return pl.pallas_call(
        functools.partial(columns_kernel, src.shape[0] - 2),
        grid_spec=pltpu.PrefetchScalarGridSpec(
            num_scalar_prefetch=1,
            grid=(),
            in_specs=[pl.BlockSpec(memory_space=pl.ANY)],
            out_specs=pl.BlockSpec(memory_space=pltpu.VMEM),
            scratch_shapes=[pltpu.SemaphoreType.DMA((2,))],
        ),
        out_shape=pltpu.VMEM((2, weight.shape[0], depth), BF16),
        cost_estimate=SMALL,
        compiler_params=pltpu.CompilerParams(vmem_limit_bytes=VMEM_LIMIT),
    )(src, in_hbm(weight))


def last_kernel(*refs):
    blocks = refs[:4]
    weight_ref, silu_ref, proj_ref, before_ref, high_ref, low_ref, out_ref, lefts, ups, sems = refs[4:]
    half, tile = lefts.shape[1], ups.shape[2]
    copies = [
        pltpu.make_async_copy(block, lefts.at[i], sems.at[i]) for i, block in enumerate(blocks)
    ]
    for copy in copies:
        copy.start()
    for copy in copies:
        copy.wait()
    for i in range(ups.shape[0]):
        cols = slice(i * tile, (i + 1) * tile)
        for h in range(2):
            rows = slice(h * half, (h + 1) * half)
            grad = dot_t(lefts[2 * h], weight_ref[0, cols, :]) + dot_t(
                lefts[2 * h + 1], weight_ref[1, cols, :]
            )
            ups[i, rows, :] = (grad * silu_ref[rows, cols]).astype(BF16)
    b = before_ref[...] + projected(ups, proj_ref)
    b_high = b.astype(BF16)
    b_low = (b - b_high.astype(F32)).astype(BF16)
    kos = b.shape[1]
    sums = jnp.dot(
        high_ref[...], jnp.concatenate([b_high, b_low], axis=1), preferred_element_type=F32
    )
    rest = jnp.dot(low_ref[...], b_high, preferred_element_type=F32)
    out_ref[...] = spread(sums[:, :kos] + (sums[:, kos:] + rest), out_ref.shape[0])


def last_step(blocks, columns, silu, proj_up, b_up, up, pairs):
    half, depth = blocks[0].shape
    tokens, hidden = silu.shape
    tile, kos = tile_of(hidden), proj_up.shape[0]
    whole = pl.BlockSpec(memory_space=pltpu.VMEM)
    ins = [in_vmem(x) for x in (columns, silu, proj_up, b_up, *up)]
    return pl.pallas_call(
        last_kernel,
        in_specs=[pl.BlockSpec(memory_space=pl.ANY)] * 4 + [whole] * len(ins),
        out_specs=whole,
        out_shape=jax.ShapeDtypeStruct((pairs, up[0].shape[0] // pairs * kos), F32),
        scratch_shapes=[
            pltpu.VMEM((4, half, depth), BF16),
            pltpu.VMEM((hidden // tile, tokens, tile), BF16),
            pltpu.SemaphoreType.DMA((4,)),
        ],
        cost_estimate=SMALL,
        compiler_params=pltpu.CompilerParams(vmem_limit_bytes=VMEM_LIMIT),
    )(*[in_hbm(x) for x in blocks], *ins)


def own_kernel(gate_ref, up_ref, down_ref, silu_ref, out_ref, hidden):
    step, tile = pl.program_id(0), gate_ref.shape[1]
    gate = gate_ref[...].astype(F32)
    silu = gate / (1.0 + jnp.exp(-gate))
    silu_ref[...] = silu
    hidden[step] = (silu * up_ref[...].astype(F32)).astype(BF16)

    @pl.when(step == hidden.shape[0] - 1)
    def _():
        total = None
        for i in range(hidden.shape[0]):
            part = dot_t(down_ref[:, i * tile : (i + 1) * tile], hidden[i])
            total = part if total is None else total + part
        out_ref[...] = total


def own_parts(gate, up, in_down):
    tokens, units = gate.shape
    tile, kis = tile_of(units), in_down.shape[0]
    tiles = pl.BlockSpec((tokens, tile), lambda i: (0, i))
    return pl.pallas_call(
        own_kernel,
        grid=(units // tile,),
        in_specs=[tiles, tiles, pl.BlockSpec((kis, units), lambda i: (0, 0))],
        out_specs=(tiles, pl.BlockSpec((kis, tokens), lambda i: (0, 0))),
        out_shape=(pltpu.HBM((tokens, units), F32), jax.ShapeDtypeStruct((kis, tokens), F32)),
        scratch_shapes=[pltpu.VMEM((units // tile, tokens, tile), BF16)],
        cost_estimate=SMALL,
        compiler_params=pltpu.CompilerParams(vmem_limit_bytes=VMEM_LIMIT),
    )(in_hbm(gate), in_hbm(up), in_down)


def turned(q, kos):
    asked, size = q.shape[0], q.shape[1] // 2
    kis = size // kos

    def kernel(q_ref, out_ref, rows):
        rows[...] = q_ref[...].astype(F32).T
        for j in range(kis):
            out_ref[j * kos : (j + 1) * kos, :] = rows[pl.ds(j, kos, stride=kis), :].astype(BF16)

    return pl.pallas_call(
        kernel,
        grid=(2,),
        in_specs=[pl.BlockSpec((asked, size), lambda i: (0, i))],
        out_specs=pl.BlockSpec((size, asked), lambda i: (i, 0)),
        out_shape=jax.ShapeDtypeStruct((2 * size, asked), BF16),
        scratch_shapes=[pltpu.VMEM((size, asked), F32)],
        cost_estimate=SMALL,
        compiler_params=pltpu.CompilerParams(vmem_limit_bytes=VMEM_LIMIT),
    )(in_hbm(q))


def score_kernel(down_ref, up_ref, q_ref, out_ref):
    size = down_ref.shape[1]
    out_ref[...] = jnp.dot(
        down_ref[...].astype(BF16), q_ref[:size, :], preferred_element_type=F32
    ) + jnp.dot(up_ref[...].astype(BF16), q_ref[size:, :], preferred_element_type=F32)


def score(down, up, q):
    return pl.pallas_call(
        score_kernel,
        out_shape=jax.ShapeDtypeStruct((down.shape[0], q.shape[1]), F32),
        cost_estimate=SMALL,
        compiler_params=pltpu.CompilerParams(vmem_limit_bytes=VMEM_LIMIT),
    )(down, up, q)


def weighted(weight, a):
    left = jnp.concatenate([weight * a[j : j + 1, :] for j in range(a.shape[0])], axis=0)
    high = left.astype(BF16)
    return high, (left - high.astype(F32)).astype(BF16)


def spread(sums, pairs):
    return jnp.concatenate([sums[r : r + pairs] for r in range(0, sums.shape[0], pairs)], axis=1)


def first_kernel(core_ref, acts_ref, grad_ref, in_up_ref, columns_ref, keep_ref, give_ref):
    first = core_ref[0] == 0
    a, b = dot_t(in_up_ref[...], acts_ref[...]), dot_t(columns_ref[...], grad_ref[...])
    half = a.shape[0] // 2
    for rows, x in ((slice(0, half), a), (slice(half, 2 * half), b)):
        keep_ref[rows, :] = jnp.where(first, x[:half], x[half:])
        give_ref[rows, :] = jnp.where(first, x[half:], x[:half])


def first_parts(core, acts, grad, in_up, columns):
    shape = jax.ShapeDtypeStruct((in_up.shape[0], acts.shape[0]), F32)
    whole = pl.BlockSpec(memory_space=pltpu.VMEM)
    return pl.pallas_call(
        first_kernel,
        in_specs=[pl.BlockSpec(memory_space=pltpu.SMEM)] + [whole] * 4,
        out_specs=(whole, whole),
        out_shape=(shape, shape),
        cost_estimate=SMALL,
        compiler_params=pltpu.CompilerParams(vmem_limit_bytes=VMEM_LIMIT),
    )(core, acts, grad, in_up, columns)


def pack_kernel(mine_ref, other_ref, part_ref):
    rows, tokens = mine_ref.shape
    depth = part_ref.shape[1]
    for c in range(tokens // depth):
        cols = slice(c * depth, (c + 1) * depth)
        part_ref[c * rows : (c + 1) * rows, :] = (mine_ref[:, cols] + other_ref[:, cols]).astype(BF16)


def packed(mine, other, depth):
    return pl.pallas_call(
        pack_kernel,
        out_shape=jax.ShapeDtypeStruct((mine.size // depth, depth), BF16),
        cost_estimate=SMALL,
        compiler_params=pltpu.CompilerParams(vmem_limit_bytes=VMEM_LIMIT),
    )(mine, other)


def pair_kernel(core_ref, weight_ref, mine_ref, other_ref, a_ref, high_ref, low_ref, out_ref):
    first, mine, other = core_ref[0] == 0, mine_ref[...], other_ref[...]
    low_half, high_half = jnp.where(first, mine, other), jnp.where(first, other, mine)
    half = mine.shape[0] // 2
    a_up = jnp.concatenate([low_half[:half], high_half[:half]], axis=0)
    b_down = jnp.concatenate([low_half[half:], high_half[half:]], axis=0)
    weight = weight_ref[...]
    high_ref[...], low_ref[...] = weighted(weight, a_up)
    b_high = b_down.astype(BF16)
    b_low = (b_down - b_high.astype(F32)).astype(BF16)
    high, low = weighted(weight, a_ref[...])
    sums = dot_t(high, b_high) + (dot_t(high, b_low) + dot_t(low, b_high))
    out_ref[...] = spread(sums, weight.shape[0])


def pair_parts(core, weight, mine, other, a_down):
    pairs, tokens = weight.shape
    kis, kos = a_down.shape[0], mine.shape[0]
    shape = pltpu.VMEM((pairs * kis, tokens), BF16)
    whole = pl.BlockSpec(memory_space=pltpu.VMEM)
    return pl.pallas_call(
        pair_kernel,
        in_specs=[pl.BlockSpec(memory_space=pltpu.SMEM)] + [whole] * 4,
        out_specs=(whole, whole, whole),
        out_shape=(shape, shape, jax.ShapeDtypeStruct((pairs, kis * kos), F32)),
        cost_estimate=SMALL,
        compiler_params=pltpu.CompilerParams(vmem_limit_bytes=VMEM_LIMIT),
    )(core, weight, mine, other, a_down)


def gathered_kernel(*refs):
    total = refs[0][...].astype(F32)
    for ref in refs[1:-1]:
        total = total + ref[...].astype(F32)
    (kis, tokens), depth = refs[-1].shape, total.shape[1]
    for c in range(tokens // depth):
        refs[-1][:, c * depth : (c + 1) * depth] = total[c * kis : (c + 1) * kis]


def gathered_sum(parts, kis, tokens):
    return pl.pallas_call(
        gathered_kernel,
        out_shape=jax.ShapeDtypeStruct((kis, tokens), F32),
        cost_estimate=SMALL,
        compiler_params=pltpu.CompilerParams(vmem_limit_bytes=VMEM_LIMIT),
    )(*parts)


def swap(value, bit, devices):
    return lax.ppermute(value, "tensor", [(i, i ^ bit) for i in range(devices)])


def per_device(
    devices,
    activations,
    gate_pre,
    up_pre,
    out_grad,
    down_weight,
    in_proj_down,
    out_proj_down,
    in_proj_up,
    out_proj_up,
    segments,
    labels,
    queries,
):
    tokens, depth = out_grad.shape
    me = lax.axis_index("tensor")
    chips = devices // 2
    ring = ring_of(chips)
    far = chips // 2
    place = {chip: i for i, chip in enumerate(ring)}

    table = np.zeros((devices, devices), np.int32)
    for device in range(devices):
        chip, core = divmod(device, 2)
        order = [chip]
        for step in range(1, far):
            order += [ring[(place[chip] - step) % chips], ring[(place[chip] + step) % chips]]
        order.append(ring[(place[chip] + far) % chips])
        table[device] = [2 * c + k for c in order for k in (core, 1 - core)]
    src = lax.dynamic_index_in_dim(jnp.asarray(table), me, 0, keepdims=False)

    ahead = [
        (2 * ring[i] + core, 2 * ring[(i + 1) % chips] + core) for i in range(chips) for core in (0, 1)
    ]
    back = [(b, a) for a, b in ahead]

    pin = lax.optimization_barrier
    kis, kos = in_proj_up.shape[0], out_proj_up.shape[0]
    seq_count = labels.shape[0]
    pairs, half = seq_count // 2, tokens // 2

    core = (me % 2)[None]

    core = (me % 2)[None]

    def send(forward, backward):
        return lax.ppermute(forward, "tensor", ahead), lax.ppermute(backward, "tensor", back)

    f, b = send(out_grad, out_grad)
    other = swap(out_grad, 1, devices)
    own_columns = lax.dynamic_slice_in_dim(out_proj_down, me * depth, depth, axis=1)
    keep, give = first_parts(core, activations, out_grad, in_proj_up, own_columns)
    part = packed(keep, swap(give, 1, devices), depth)
    gate_pre, up_pre, part = pin((gate_pre, up_pre, part))
    silu_gate, a_down = own_parts(gate_pre, up_pre, in_proj_down)
    part, a_down = pin((part, a_down))
    part_f, part_b = send(part, part)
    seqs = jnp.arange(seq_count, dtype=jnp.int32)[:, None]
    signs = (2 * labels - 1).astype(F32)
    per_seq = jnp.where(segments[None, :] == seqs, signs[:, None], F32(0.0))
    pair_weight = per_seq.reshape(pairs, 2, tokens).sum(axis=1)

    def halves(array, place):
        return [(array, 0, place), (array, 1, place)]

    f, b, part_f, part_b, other, a_down, pair_weight = pin(
        (f, b, part_f, part_b, other, a_down, pair_weight)
    )
    known, parts, came = None, [part, part_f, part_b], (f, b)
    units = [halves(out_grad, 0), halves(other, 1)]
    for step in range(1, far):
        if step < far - 1:
            f, b = send(f, b)
            part_f, part_b = send(part_f, part_b)
            parts += [part_f, part_b]
            if step == 1:
                part_far = lax.ppermute(
                    part,
                    "tensor",
                    [
                        (2 * ring[i] + k, 2 * ring[(i + far) % chips] + k)
                        for i in range(chips)
                        for k in (0, 1)
                    ],
                )
                parts.append(part_far)
        else:
            f, b = send(f[:half], b[half:])
        place = 4 * step - 2
        for i, array in enumerate(came):
            units += [
                halves(array, place + 2 * i),
                halves(swap(array, 1, devices), place + 2 * i + 1),
            ]
        if step == far - 2:
            columns, q_turned = last_columns(src, down_weight, depth), turned(queries, kos)
            src, columns, q_turned = pin((src, columns, q_turned))
        if step == far - 1:
            mine = gathered_sum(parts, kis, tokens)
            high, low, down = pair_parts(core, pair_weight, mine, swap(mine, 1, devices), a_down)
            src, high, low, down = pin((src, high, low, down))
            b_up = b_step(src, half, units, down_weight, known, silu_gate, out_proj_up)
        else:
            known = add_step(src, half, units, down_weight, known)
            units = []
            f, b, part_f, part_b, parts, known = pin((f, b, part_f, part_b, parts, known))
            came = (f, b)
    f, b, b_up, high, low, down = pin((f, b, b_up, high, low, down))
    blocks = [x for block in (f, b) for x in (block, swap(block, 1, devices))]
    up = last_step(blocks, columns, silu_gate, out_proj_up, b_up, (high, low), pairs)

    first = core == 0
    total = jnp.where(first, down, up) + swap(jnp.where(first, up, down), 1, devices)
    for bit in range(1, devices.bit_length() - 1):
        total = total + swap(total.astype(BF16), 1 << bit, devices).astype(F32)
    theirs = swap(total, 1, devices)
    return score(jnp.where(first, total, theirs), jnp.where(first, theirs, total), q_turned)


def solution(mesh):
    in_specs = (
        P("groups", "tensor"),
        P("groups", "tensor"),
        P("groups", "tensor"),
        P("groups", "tensor"),
        P("tensor", None),
        P(None, "tensor"),
        P(),
        P(None, "tensor"),
        P(None, "tensor"),
        P("groups"),
        P("groups"),
        P("tensor", None),
    )
    return jax.shard_map(
        functools.partial(per_device, mesh.shape["tensor"]),
        mesh=mesh,
        in_specs=in_specs,
        out_specs=P("groups", "tensor"),
        check_vma=False,
    )
```

```python
import functools

import jax
import jax.numpy as jnp
import numpy as np
from jax import lax
from jax.experimental import pallas as pl
from jax.experimental.pallas import tpu as pltpu
from jax.sharding import PartitionSpec as P

F32, BF16 = jnp.float32, jnp.bfloat16
VMEM_LIMIT = 24 * 1024 * 1024
SMALL = pl.CostEstimate(flops=1000, bytes_accessed=1000, transcendentals=0)


def dot_t(left, right, precision=None):
    return lax.dot_general(
        left, right, (((1,), (1,)), ((), ())), preferred_element_type=F32, precision=precision
    )


def ring_of(chips):
    if chips == 8:
        return [0, 2, 4, 6, 7, 5, 3, 1]
    return list(range(chips))


def tile_of(units):
    return 256 if units % 256 == 0 else units


def products(lefts, weights):
    total = None
    for i, weight in enumerate(weights):
        part = dot_t(lefts[i], weight[...])
        total = part if total is None else total + part
    return total


def load(blocks, lefts, sems):
    half = lefts.shape[1] // 2
    copies = []
    for i, (array, row) in enumerate(blocks):
        rows = pl.ds((i % 2) * half, half)
        source = array.at[pl.ds(row * half, half)]
        copies.append(pltpu.make_async_copy(source, lefts.at[i // 2, rows], sems.at[i]))
    for copy in copies:
        copy.start()
    for copy in copies:
        copy.wait()


def step_kernel(count, src_ref, *refs):
    blocks, weights = refs[:count], refs[count : 2 * count]
    out_ref, lefts, sems = refs[-3:]
    before_ref = refs[2 * count] if len(refs) == 2 * count + 4 else None
    step = pl.program_id(0)

    @pl.when(step == 0)
    def _():
        load([(block, i) for block in blocks for i in range(2)], lefts, sems)

    total = products(lefts, weights)
    out_ref[step] = total if before_ref is None else total + before_ref[step]


def projected(ups, proj_ref):
    total, tile = None, ups.shape[2]
    for i in range(ups.shape[0]):
        part = dot_t(ups[i], proj_ref[:, i * tile : (i + 1) * tile])
        total = part if total is None else total + part
    return total


def in_hbm(x):
    return pltpu.with_memory_space_constraint(x, pltpu.HBM)


def in_vmem(x):
    return pltpu.with_memory_space_constraint(x, pltpu.VMEM)


ANYWHERE = pl.BlockSpec(memory_space=pl.ANY)
WHOLE = pl.BlockSpec(memory_space=pltpu.VMEM)


def step_parts(units, weight):
    tokens, depth = units[0][0].shape
    tile = tile_of(weight.shape[0])
    ins = [in_hbm(array) for array, _ in units] + [in_hbm(weight)] * len(units)
    specs = [ANYWHERE] * len(units)
    specs += [pl.BlockSpec((tile, depth), lambda i, s, m=m: (i, s[m])) for _, m in units]
    scratch = [
        pltpu.VMEM((len(units), tokens, depth), BF16),
        pltpu.SemaphoreType.DMA((2 * len(units),)),
    ]
    return ins, specs, scratch, tile


def add_step(src, units, weight, before):
    ins, specs, scratch, tile = step_parts(units, weight)
    tokens, hidden = units[0][0].shape[0], weight.shape[0]
    aliases = {}
    if before is not None:
        ins.append(in_vmem(before))
        specs.append(WHOLE)
        aliases = {len(ins): 0}
    return pl.pallas_call(
        functools.partial(step_kernel, len(units)),
        grid_spec=pltpu.PrefetchScalarGridSpec(
            num_scalar_prefetch=1,
            grid=(hidden // tile,),
            in_specs=specs,
            out_specs=WHOLE,
            scratch_shapes=scratch,
        ),
        out_shape=pltpu.VMEM((hidden // tile, tokens, tile), F32),
        input_output_aliases=aliases,
        cost_estimate=SMALL,
        compiler_params=pltpu.CompilerParams(vmem_limit_bytes=VMEM_LIMIT),
    )(src, *ins)


def columns_kernel(first, src_ref, weight_ref, out_ref, sems):
    depth = out_ref.shape[2]
    copies = []
    for m in range(2):
        start = pl.multiple_of(src_ref[first + m] * depth, depth)
        copies.append(
            pltpu.make_async_copy(weight_ref.at[:, pl.ds(start, depth)], out_ref.at[m], sems.at[m])
        )
    for copy in copies:
        copy.start()
    for copy in copies:
        copy.wait()


def last_columns(src, weight, depth):
    return pl.pallas_call(
        functools.partial(columns_kernel, src.shape[0] - 2),
        grid_spec=pltpu.PrefetchScalarGridSpec(
            num_scalar_prefetch=1,
            grid=(),
            in_specs=[pl.BlockSpec(memory_space=pl.ANY)],
            out_specs=pl.BlockSpec(memory_space=pltpu.VMEM),
            scratch_shapes=[pltpu.SemaphoreType.DMA((2,))],
        ),
        out_shape=pltpu.VMEM((2, weight.shape[0], depth), BF16),
        cost_estimate=SMALL,
        compiler_params=pltpu.CompilerParams(vmem_limit_bytes=VMEM_LIMIT),
    )(src, in_hbm(weight))


def last_kernel(*refs):
    blocks = refs[:4]
    weight_ref, silu_ref, proj_ref, before_ref, high_ref, low_ref, out_ref, lefts, ups, sems = refs[4:]
    half, tile = lefts.shape[1] // 2, ups.shape[2]
    load([(block, 0) for block in (blocks[0], blocks[2], blocks[1], blocks[3])], lefts, sems)
    for i in range(ups.shape[0]):
        cols = slice(i * tile, (i + 1) * tile)
        for h in range(2):
            rows = slice(h * half, (h + 1) * half)
            grad = dot_t(lefts[0, rows, :], weight_ref[0, cols, :]) + dot_t(
                lefts[1, rows, :], weight_ref[1, cols, :]
            )
            grad = grad + before_ref[i, rows, :]
            ups[i, rows, :] = (grad * silu_ref[i, rows, :]).astype(BF16)
    b_high, b_low = parts_of(projected(ups, proj_ref))
    kos = b_high.shape[1]
    sums = jnp.dot(
        high_ref[...], jnp.concatenate([b_high, b_low], axis=1), preferred_element_type=F32
    )
    rest = jnp.dot(low_ref[...], b_high, preferred_element_type=F32)
    out_ref[...] = spread(sums[:, :kos] + (sums[:, kos:] + rest), out_ref.shape[0])


def last_step(blocks, columns, silu, proj_up, before, up, pairs):
    half, depth = blocks[0].shape
    tiles, tokens, tile = silu.shape
    kos = proj_up.shape[0]
    ins = [in_vmem(x) for x in (columns, silu, proj_up, before, *up)]
    return pl.pallas_call(
        last_kernel,
        in_specs=[ANYWHERE] * 4 + [WHOLE] * len(ins),
        out_specs=WHOLE,
        out_shape=jax.ShapeDtypeStruct((pairs, up[0].shape[0] // pairs * kos), F32),
        scratch_shapes=[
            pltpu.VMEM((2, tokens, depth), BF16),
            pltpu.VMEM((tiles, tokens, tile), BF16),
            pltpu.SemaphoreType.DMA((4,)),
        ],
        cost_estimate=SMALL,
        compiler_params=pltpu.CompilerParams(vmem_limit_bytes=VMEM_LIMIT),
    )(*[in_hbm(x) for x in blocks], *ins)


def own_kernel(gate_ref, up_ref, down_ref, silu_ref, out_ref, hidden):
    step, tile = pl.program_id(0), gate_ref.shape[1]
    gate = gate_ref[...].astype(F32)
    silu = gate / (1.0 + jnp.exp(-gate))
    silu_ref[step] = silu
    hidden[step] = (silu * up_ref[...].astype(F32)).astype(BF16)

    @pl.when(step == hidden.shape[0] - 1)
    def _():
        total = None
        for i in range(hidden.shape[0]):
            part = dot_t(down_ref[:, i * tile : (i + 1) * tile], hidden[i])
            total = part if total is None else total + part
        out_ref[...] = total


def own_parts(gate, up, in_down):
    tokens, units = gate.shape
    tile, kis = tile_of(units), in_down.shape[0]
    tiles = pl.BlockSpec((tokens, tile), lambda i: (0, i))
    return pl.pallas_call(
        own_kernel,
        grid=(units // tile,),
        in_specs=[tiles, tiles, pl.BlockSpec((kis, units), lambda i: (0, 0))],
        out_specs=(WHOLE, pl.BlockSpec((kis, tokens), lambda i: (0, 0))),
        out_shape=(
            pltpu.VMEM((units // tile, tokens, tile), F32),
            jax.ShapeDtypeStruct((kis, tokens), F32),
        ),
        scratch_shapes=[pltpu.VMEM((units // tile, tokens, tile), BF16)],
        cost_estimate=SMALL,
        compiler_params=pltpu.CompilerParams(vmem_limit_bytes=VMEM_LIMIT),
    )(in_hbm(gate), in_hbm(up), in_down)


def turned(q, kos):
    asked, size = q.shape[0], q.shape[1] // 2
    kis = size // kos

    def kernel(q_ref, out_ref, rows):
        rows[...] = q_ref[...].astype(F32).T
        for j in range(kis):
            out_ref[j * kos : (j + 1) * kos, :] = rows[pl.ds(j, kos, stride=kis), :].astype(BF16)

    return pl.pallas_call(
        kernel,
        grid=(2,),
        in_specs=[pl.BlockSpec((asked, size), lambda i: (0, i))],
        out_specs=pl.BlockSpec((size, asked), lambda i: (i, 0)),
        out_shape=jax.ShapeDtypeStruct((2 * size, asked), BF16),
        scratch_shapes=[pltpu.VMEM((size, asked), F32)],
        cost_estimate=SMALL,
        compiler_params=pltpu.CompilerParams(vmem_limit_bytes=VMEM_LIMIT),
    )(in_hbm(q))


def score_kernel(down_ref, up_ref, q_ref, out_ref):
    pairs, size = down_ref.shape
    total = None
    for i, ref in enumerate((down_ref, up_ref)):
        both = jnp.concatenate(parts_of(ref[...]), axis=0)
        part = jnp.dot(both, q_ref[i * size : (i + 1) * size, :], preferred_element_type=F32)
        total = part if total is None else total + part
    out_ref[...] = total[:pairs] + total[pairs:]


def score(down, up, q):
    return pl.pallas_call(
        score_kernel,
        out_shape=jax.ShapeDtypeStruct((down.shape[0], q.shape[1]), F32),
        cost_estimate=SMALL,
        compiler_params=pltpu.CompilerParams(vmem_limit_bytes=VMEM_LIMIT),
    )(down, up, q)


def parts_of(x):
    high = x.astype(BF16)
    return high, (x - high.astype(F32)).astype(BF16)


def weighted(weight, a):
    return parts_of(jnp.concatenate([weight * a[j : j + 1, :] for j in range(a.shape[0])], axis=0))


def spread(sums, pairs):
    return jnp.concatenate([sums[r : r + pairs] for r in range(0, sums.shape[0], pairs)], axis=1)


def first_kernel(core_ref, acts_ref, grad_ref, in_up_ref, columns_ref, keep_ref, give_ref):
    first = core_ref[0] == 0
    a, b = dot_t(in_up_ref[...], acts_ref[...]), dot_t(columns_ref[...], grad_ref[...])
    half = a.shape[0] // 2
    for rows, x in ((slice(0, half), a), (slice(half, 2 * half), b)):
        keep_ref[rows, :] = jnp.where(first, x[:half], x[half:])
        give_ref[rows, :] = jnp.where(first, x[half:], x[:half])


def first_parts(core, acts, grad, in_up, columns):
    shape = jax.ShapeDtypeStruct((in_up.shape[0], acts.shape[0]), F32)
    whole = pl.BlockSpec(memory_space=pltpu.VMEM)
    return pl.pallas_call(
        first_kernel,
        in_specs=[pl.BlockSpec(memory_space=pltpu.SMEM)] + [whole] * 4,
        out_specs=(whole, whole),
        out_shape=(shape, shape),
        cost_estimate=SMALL,
        compiler_params=pltpu.CompilerParams(vmem_limit_bytes=VMEM_LIMIT),
    )(core, acts, grad, in_up, columns)


def pair_kernel(place_ref, weight_ref, mine_ref, across_ref, mine1_ref, across1_ref, a_ref, high_ref, low_ref, out_ref):
    first, near = place_ref[0] == 0, place_ref[1] == 0
    rows = []
    for mine, across in ((mine_ref, across_ref), (mine1_ref, across1_ref)):
        mine, across = mine[...], across[...]
        rows.append((jnp.where(near, mine, across), jnp.where(near, across, mine)))
    (a0, b0), (a1, b1) = rows
    a_up = jnp.concatenate([jnp.where(first, a0, a1), jnp.where(first, a1, a0)], axis=0)
    b_down = jnp.concatenate([jnp.where(first, b0, b1), jnp.where(first, b1, b0)], axis=0)
    weight = weight_ref[...]
    high_ref[...], low_ref[...] = weighted(weight, a_up)
    b_high, b_low = parts_of(b_down)
    high, low = weighted(weight, a_ref[...])
    sums = dot_t(high, b_high) + (dot_t(high, b_low) + dot_t(low, b_high))
    out_ref[...] = spread(sums, weight.shape[0])


def pair_parts(place, weight, quarters, a_down):
    pairs, tokens = weight.shape
    kis, kos = a_down.shape[0], 2 * quarters[0].shape[0]
    shape = pltpu.VMEM((pairs * kis, tokens), BF16)
    return pl.pallas_call(
        pair_kernel,
        in_specs=[pl.BlockSpec(memory_space=pltpu.SMEM)] + [WHOLE] * 6,
        out_specs=(WHOLE, WHOLE, WHOLE),
        out_shape=(shape, shape, jax.ShapeDtypeStruct((pairs, kis * kos), F32)),
        cost_estimate=SMALL,
        compiler_params=pltpu.CompilerParams(vmem_limit_bytes=VMEM_LIMIT),
    )(place, weight, *quarters, a_down)


def swap(value, bit, devices):
    return lax.ppermute(value, "tensor", [(i, i ^ bit) for i in range(devices)])


def per_device(
    devices,
    activations,
    gate_pre,
    up_pre,
    out_grad,
    down_weight,
    in_proj_down,
    out_proj_down,
    in_proj_up,
    out_proj_up,
    segments,
    labels,
    queries,
):
    tokens, depth = out_grad.shape
    me = lax.axis_index("tensor")
    chips = devices // 2
    ring = ring_of(chips)
    far = chips // 2
    place = {chip: i for i, chip in enumerate(ring)}

    table = np.zeros((devices, devices), np.int32)
    for device in range(devices):
        chip, core = divmod(device, 2)
        order = [chip]
        for step in range(1, far):
            order += [ring[(place[chip] - step) % chips], ring[(place[chip] + step) % chips]]
        order.append(ring[(place[chip] + far) % chips])
        table[device] = [2 * c + k for c in order for k in (core, 1 - core)]
    src = lax.dynamic_index_in_dim(jnp.asarray(table), me, 0, keepdims=False)

    ahead = [
        (2 * ring[i] + core, 2 * ring[(i + 1) % chips] + core) for i in range(chips) for core in (0, 1)
    ]
    back = [(b, a) for a, b in ahead]

    pin = lax.optimization_barrier
    kis, kos = in_proj_up.shape[0], out_proj_up.shape[0]
    seq_count = labels.shape[0]
    pairs, half = seq_count // 2, tokens // 2

    core = (me % 2)[None]

    def send(forward, backward):
        return lax.ppermute(forward, "tensor", ahead), lax.ppermute(backward, "tensor", back)

    f, b = send(out_grad, out_grad)
    other = swap(out_grad, 1, devices)
    own_columns = lax.dynamic_slice_in_dim(out_proj_down, me * depth, depth, axis=1)
    keep, give = first_parts(core, activations, out_grad, in_proj_up, own_columns)
    part = keep + swap(give, 1, devices)
    gate_pre, up_pre, part = pin((gate_pre, up_pre, part))
    silu_gate, a_down = own_parts(gate_pre, up_pre, in_proj_down)
    bits = [1 << i for i in range(2, devices.bit_length() - 1)]
    rounds = [[]] + [[int(bit) for bit in some] for some in np.array_split(bits, far - 2)]
    row = part.shape[0] // 2
    side = (me // 2) % 2
    give = lax.dynamic_slice_in_dim(part, (1 - side) * row, row, axis=0)
    part = lax.dynamic_slice_in_dim(part, side * row, row, axis=0)

    def ask(part, step):
        return [swap(part.astype(BF16), bit, devices) for bit in rounds[step]]

    def added(part, theirs):
        for more in theirs:
            part = part + more.astype(F32)
        return part

    theirs = [swap(give.astype(BF16), 2, devices)]
    seqs = jnp.arange(seq_count, dtype=jnp.int32)[:, None]
    signs = (2 * labels - 1).astype(F32)
    per_seq = jnp.where(segments[None, :] == seqs, signs[:, None], F32(0.0))
    pair_weight = per_seq.reshape(pairs, 2, tokens).sum(axis=1)

    f, b, theirs, other, a_down, pair_weight = pin((f, b, theirs, other, a_down, pair_weight))
    part = added(part, theirs)
    known, came = None, (f, b)
    units = [(out_grad, 0), (other, 1)]
    for step in range(1, far):
        if step < far - 1:
            f, b = send(f, b)
            theirs = ask(part, step)
        else:
            f, b = send(f[:half], b[half:])
        place = 4 * step - 2
        for i, array in enumerate(came):
            units += [(array, place + 2 * i), (swap(array, 1, devices), place + 2 * i + 1)]
        if step == far - 2:
            columns, q_turned = last_columns(src, down_weight, depth), turned(queries, kos)
            src, columns, q_turned = pin((src, columns, q_turned))
        if step == far - 1:
            known = add_step(src, units, down_weight, known)
            across = swap(part, 2, devices)
            known, part, across = pin((known, part, across))
            high, low, down = pair_parts(
                jnp.stack([me % 2, side]),
                pair_weight,
                (part, across, swap(part, 1, devices), swap(across, 1, devices)),
                a_down,
            )
        else:
            known = add_step(src, units, down_weight, known)
            units = []
            f, b, theirs, known = pin((f, b, theirs, known))
            part = added(part, theirs)
            came = (f, b)
    f, b, known = pin((f, b, known))
    blocks = [x for block in (f, b) for x in (block, swap(block, 1, devices))]
    up = last_step(blocks, columns, silu_gate, out_proj_up, known, (high, low), pairs)

    first = core == 0
    total = jnp.where(first, down, up) + swap(jnp.where(first, up, down), 1, devices)
    for bit in range(1, devices.bit_length() - 1):
        if bit < 3:
            total = total + swap(total, 1 << bit, devices)
        else:
            total = total + swap(total.astype(BF16), 1 << bit, devices).astype(F32)
    rest = swap(total, 1, devices)
    return score(jnp.where(first, total, rest), jnp.where(first, rest, total), q_turned)


def solution(mesh):
    in_specs = (
        P("groups", "tensor"),
        P("groups", "tensor"),
        P("groups", "tensor"),
        P("groups", "tensor"),
        P("tensor", None),
        P(None, "tensor"),
        P(),
        P(None, "tensor"),
        P(None, "tensor"),
        P("groups"),
        P("groups"),
        P("tensor", None),
    )
    return jax.shard_map(
        functools.partial(per_device, mesh.shape["tensor"]),
        mesh=mesh,
        in_specs=in_specs,
        out_specs=P("groups", "tensor"),
        check_vma=False,
    )
```

```python
import functools

import jax
import jax.numpy as jnp
import numpy as np
from jax import lax
from jax.experimental import pallas as pl
from jax.experimental.pallas import tpu as pltpu
from jax.sharding import PartitionSpec as P

F32, BF16 = jnp.float32, jnp.bfloat16
VMEM_LIMIT = 24 * 1024 * 1024
SMALL = pl.CostEstimate(flops=1000, bytes_accessed=1000, transcendentals=0)


def dot_t(left, right, precision=None):
    return lax.dot_general(
        left, right, (((1,), (1,)), ((), ())), preferred_element_type=F32, precision=precision
    )


def ring_of(chips):
    if chips == 8:
        return [0, 2, 4, 6, 7, 5, 3, 1]
    return list(range(chips))


def tile_of(units):
    return 256 if units % 256 == 0 else units


def products(lefts, weights):
    total = None
    for i, weight in enumerate(weights):
        part = dot_t(lefts[i], weight[...])
        total = part if total is None else total + part
    return total


def load(blocks, lefts, sems):
    half = lefts.shape[1] // 2
    copies = []
    for i, (array, row) in enumerate(blocks):
        rows = pl.ds((i % 2) * half, half)
        source = array.at[pl.ds(row * half, half)]
        copies.append(pltpu.make_async_copy(source, lefts.at[i // 2, rows], sems.at[i]))
    for copy in copies:
        copy.start()
    for copy in copies:
        copy.wait()


def step_kernel(count, src_ref, *refs):
    blocks, weights = refs[:count], refs[count : 2 * count]
    out_ref, lefts, sems = refs[-3:]
    before_ref = refs[2 * count] if len(refs) == 2 * count + 4 else None
    step = pl.program_id(0)

    @pl.when(step == 0)
    def _():
        load([(block, i) for block in blocks for i in range(2)], lefts, sems)

    total = products(lefts, weights)
    out_ref[step] = total if before_ref is None else total + before_ref[step]


def projected(ups, proj_ref):
    total, tile = None, ups.shape[2]
    for i in range(ups.shape[0]):
        part = dot_t(ups[i], proj_ref[:, i * tile : (i + 1) * tile])
        total = part if total is None else total + part
    return total


def in_hbm(x):
    return pltpu.with_memory_space_constraint(x, pltpu.HBM)


def in_vmem(x):
    return pltpu.with_memory_space_constraint(x, pltpu.VMEM)


ANYWHERE = pl.BlockSpec(memory_space=pl.ANY)
WHOLE = pl.BlockSpec(memory_space=pltpu.VMEM)


def step_parts(units, weight):
    tokens, depth = units[0][0].shape
    tile = tile_of(weight.shape[0])
    ins = [in_hbm(array) if place == 0 else array for array, place in units]
    ins += [in_hbm(weight)] * len(units)
    specs = [ANYWHERE] * len(units)
    specs += [pl.BlockSpec((tile, depth), lambda i, s, m=m: (i, s[m])) for _, m in units]
    scratch = [
        pltpu.VMEM((len(units), tokens, depth), BF16),
        pltpu.SemaphoreType.DMA((2 * len(units),)),
    ]
    return ins, specs, scratch, tile


def add_step(src, units, weight, before):
    ins, specs, scratch, tile = step_parts(units, weight)
    tokens, hidden = units[0][0].shape[0], weight.shape[0]
    aliases = {}
    if before is not None:
        ins.append(in_vmem(before))
        specs.append(WHOLE)
        aliases = {len(ins): 0}
    return pl.pallas_call(
        functools.partial(step_kernel, len(units)),
        grid_spec=pltpu.PrefetchScalarGridSpec(
            num_scalar_prefetch=1,
            grid=(hidden // tile,),
            in_specs=specs,
            out_specs=WHOLE,
            scratch_shapes=scratch,
        ),
        out_shape=pltpu.VMEM((hidden // tile, tokens, tile), F32),
        input_output_aliases=aliases,
        cost_estimate=SMALL,
        compiler_params=pltpu.CompilerParams(vmem_limit_bytes=VMEM_LIMIT),
    )(src, *ins)


def columns_kernel(places, src_ref, weight_ref, out_ref, sems):
    depth = out_ref.shape[2]
    copies = []
    for i, place in enumerate(places):
        start = pl.multiple_of(src_ref[place] * depth, depth)
        copies.append(
            pltpu.make_async_copy(weight_ref.at[:, pl.ds(start, depth)], out_ref.at[i], sems.at[i])
        )
    for copy in copies:
        copy.start()
    for copy in copies:
        copy.wait()


def columns_of(src, weight, depth, places):
    return pl.pallas_call(
        functools.partial(columns_kernel, places),
        grid_spec=pltpu.PrefetchScalarGridSpec(
            num_scalar_prefetch=1,
            grid=(),
            in_specs=[ANYWHERE],
            out_specs=WHOLE,
            scratch_shapes=[pltpu.SemaphoreType.DMA((len(places),))],
        ),
        out_shape=pltpu.VMEM((len(places), weight.shape[0], depth), BF16),
        cost_estimate=SMALL,
        compiler_params=pltpu.CompilerParams(vmem_limit_bytes=VMEM_LIMIT),
    )(src, in_hbm(weight))


def last_kernel(*refs):
    halves = refs[:4]
    weight_ref, silu_ref, proj_ref, before_ref, high_ref, low_ref, out_ref, lefts, ups, sems = refs[4:]
    half, tile = lefts.shape[1] // 2, ups.shape[2]
    load([(halves[i], 0) for i in (0, 2, 1, 3)], lefts, sems)
    for i in range(ups.shape[0]):
        cols = slice(i * tile, (i + 1) * tile)
        for h in range(2):
            rows = slice(h * half, (h + 1) * half)
            grad = before_ref[i, rows, :]
            for m in range(lefts.shape[0]):
                grad = grad + dot_t(lefts[m, rows, :], weight_ref[m, cols, :])
            ups[i, rows, :] = (grad * silu_ref[i, rows, :]).astype(BF16)
    b_high, b_low = parts_of(projected(ups, proj_ref))
    kos = b_high.shape[1]
    sums = jnp.dot(
        high_ref[...], jnp.concatenate([b_high, b_low], axis=1), preferred_element_type=F32
    )
    rest = jnp.dot(low_ref[...], b_high, preferred_element_type=F32)
    out_ref[...] = spread(sums[:, :kos] + (sums[:, kos:] + rest), out_ref.shape[0])


def last_step(halves, columns, silu, proj_up, before, up, pairs):
    tiles, tokens, tile = silu.shape
    depth, kos = halves[0].shape[1], proj_up.shape[0]
    ins = [in_vmem(x) for x in (columns, silu, proj_up, before, *up)]
    return pl.pallas_call(
        last_kernel,
        in_specs=[ANYWHERE] * 4 + [WHOLE] * len(ins),
        out_specs=WHOLE,
        out_shape=jax.ShapeDtypeStruct((pairs, up[0].shape[0] // pairs * kos), F32),
        scratch_shapes=[
            pltpu.VMEM((2, tokens, depth), BF16),
            pltpu.VMEM((tiles, tokens, tile), BF16),
            pltpu.SemaphoreType.DMA((4,)),
        ],
        cost_estimate=SMALL,
        compiler_params=pltpu.CompilerParams(vmem_limit_bytes=VMEM_LIMIT),
    )(*halves, *ins)


def own_kernel(gate_ref, up_ref, down_ref, silu_ref, out_ref, hidden):
    step, tile = pl.program_id(0), gate_ref.shape[1]
    gate = gate_ref[...].astype(F32)
    silu = gate / (1.0 + jnp.exp(-gate))
    silu_ref[step] = silu
    hidden[step] = (silu * up_ref[...].astype(F32)).astype(BF16)

    @pl.when(step == hidden.shape[0] - 1)
    def _():
        total = None
        for i in range(hidden.shape[0]):
            part = dot_t(down_ref[:, i * tile : (i + 1) * tile], hidden[i])
            total = part if total is None else total + part
        out_ref[...] = total


def own_parts(gate, up, in_down):
    tokens, units = gate.shape
    tile, kis = tile_of(units), in_down.shape[0]
    tiles = pl.BlockSpec((tokens, tile), lambda i: (0, i))
    return pl.pallas_call(
        own_kernel,
        grid=(units // tile,),
        in_specs=[tiles, tiles, pl.BlockSpec((kis, units), lambda i: (0, 0))],
        out_specs=(WHOLE, pl.BlockSpec((kis, tokens), lambda i: (0, 0))),
        out_shape=(
            pltpu.VMEM((units // tile, tokens, tile), F32),
            jax.ShapeDtypeStruct((kis, tokens), F32),
        ),
        scratch_shapes=[pltpu.VMEM((units // tile, tokens, tile), BF16)],
        cost_estimate=SMALL,
        compiler_params=pltpu.CompilerParams(vmem_limit_bytes=VMEM_LIMIT),
    )(in_hbm(gate), in_hbm(up), in_down)


def turned(q, kos):
    asked, size = q.shape[0], q.shape[1] // 2
    kis = size // kos

    def kernel(q_ref, out_ref, rows):
        rows[...] = q_ref[...].astype(F32).T
        for j in range(kis):
            out_ref[j * kos : (j + 1) * kos, :] = rows[pl.ds(j, kos, stride=kis), :].astype(BF16)

    return pl.pallas_call(
        kernel,
        grid=(2,),
        in_specs=[pl.BlockSpec((asked, size), lambda i: (0, i))],
        out_specs=pl.BlockSpec((size, asked), lambda i: (i, 0)),
        out_shape=jax.ShapeDtypeStruct((2 * size, asked), BF16),
        scratch_shapes=[pltpu.VMEM((size, asked), F32)],
        cost_estimate=SMALL,
        compiler_params=pltpu.CompilerParams(vmem_limit_bytes=VMEM_LIMIT),
    )(in_hbm(q))


def score_kernel(down_ref, up_ref, q_ref, out_ref):
    pairs, size = down_ref.shape
    total = None
    for i, ref in enumerate((down_ref, up_ref)):
        both = jnp.concatenate(parts_of(ref[...]), axis=0)
        part = jnp.dot(both, q_ref[i * size : (i + 1) * size, :], preferred_element_type=F32)
        total = part if total is None else total + part
    out_ref[...] = total[:pairs] + total[pairs:]


def score(down, up, q):
    return pl.pallas_call(
        score_kernel,
        out_shape=jax.ShapeDtypeStruct((down.shape[0], q.shape[1]), F32),
        cost_estimate=SMALL,
        compiler_params=pltpu.CompilerParams(vmem_limit_bytes=VMEM_LIMIT),
    )(down, up, q)


def parts_of(x):
    high = x.astype(BF16)
    return high, (x - high.astype(F32)).astype(BF16)


def weighted(weight, a):
    return parts_of(jnp.concatenate([weight * a[j : j + 1, :] for j in range(a.shape[0])], axis=0))


def spread(sums, pairs):
    return jnp.concatenate([sums[r : r + pairs] for r in range(0, sums.shape[0], pairs)], axis=1)


def first_kernel(core_ref, acts_ref, grad_ref, in_up_ref, columns_ref, keep_ref, give_ref):
    first = core_ref[0] == 0
    a, b = dot_t(in_up_ref[...], acts_ref[...]), dot_t(columns_ref[...], grad_ref[...])
    half = a.shape[0] // 2
    for rows, x in ((slice(0, half), a), (slice(half, 2 * half), b)):
        keep_ref[rows, :] = jnp.where(first, x[:half], x[half:])
        give_ref[rows, :] = jnp.where(first, x[half:], x[:half])


def first_parts(core, acts, grad, in_up, columns):
    shape = jax.ShapeDtypeStruct((in_up.shape[0], acts.shape[0]), F32)
    whole = pl.BlockSpec(memory_space=pltpu.VMEM)
    return pl.pallas_call(
        first_kernel,
        in_specs=[pl.BlockSpec(memory_space=pltpu.SMEM)] + [whole] * 4,
        out_specs=(whole, whole),
        out_shape=(shape, shape),
        cost_estimate=SMALL,
        compiler_params=pltpu.CompilerParams(vmem_limit_bytes=VMEM_LIMIT),
    )(core, acts, grad, in_up, columns)


def pair_kernel(place_ref, weight_ref, mine_ref, across_ref, mine1_ref, across1_ref, a_ref, high_ref, low_ref, out_ref):
    first, near = place_ref[0] == 0, place_ref[1] == 0
    rows = []
    for mine, across in ((mine_ref, across_ref), (mine1_ref, across1_ref)):
        mine, across = mine[...], across[...]
        rows.append((jnp.where(near, mine, across), jnp.where(near, across, mine)))
    (a0, b0), (a1, b1) = rows
    a_up = jnp.concatenate([jnp.where(first, a0, a1), jnp.where(first, a1, a0)], axis=0)
    b_down = jnp.concatenate([jnp.where(first, b0, b1), jnp.where(first, b1, b0)], axis=0)
    weight = weight_ref[...]
    high_ref[...], low_ref[...] = weighted(weight, a_up)
    b_high, b_low = parts_of(b_down)
    high, low = weighted(weight, a_ref[...])
    sums = dot_t(high, b_high) + (dot_t(high, b_low) + dot_t(low, b_high))
    out_ref[...] = spread(sums, weight.shape[0])


def pair_parts(place, weight, quarters, a_down):
    pairs, tokens = weight.shape
    kis, kos = a_down.shape[0], 2 * quarters[0].shape[0]
    shape = pltpu.VMEM((pairs * kis, tokens), BF16)
    return pl.pallas_call(
        pair_kernel,
        in_specs=[pl.BlockSpec(memory_space=pltpu.SMEM)] + [WHOLE] * 6,
        out_specs=(WHOLE, WHOLE, WHOLE),
        out_shape=(shape, shape, jax.ShapeDtypeStruct((pairs, kis * kos), F32)),
        cost_estimate=SMALL,
        compiler_params=pltpu.CompilerParams(vmem_limit_bytes=VMEM_LIMIT),
    )(place, weight, *quarters, a_down)


def swap(value, bit, devices):
    return lax.ppermute(value, "tensor", [(i, i ^ bit) for i in range(devices)])


def per_device(
    devices,
    activations,
    gate_pre,
    up_pre,
    out_grad,
    down_weight,
    in_proj_down,
    out_proj_down,
    in_proj_up,
    out_proj_up,
    segments,
    labels,
    queries,
):
    tokens, depth = out_grad.shape
    me = lax.axis_index("tensor")
    chips = devices // 2
    ring = ring_of(chips)
    far = chips // 2
    place = {chip: i for i, chip in enumerate(ring)}

    table = np.zeros((devices, devices), np.int32)
    for device in range(devices):
        chip, core = divmod(device, 2)
        order = [chip]
        for step in range(1, far):
            order += [ring[(place[chip] - step) % chips], ring[(place[chip] + step) % chips]]
        order.append(ring[(place[chip] + far) % chips])
        table[device] = [2 * c + k for c in order for k in (core, 1 - core)]
    src = lax.dynamic_index_in_dim(jnp.asarray(table), me, 0, keepdims=False)

    ahead = [
        (2 * ring[i] + core, 2 * ring[(i + 1) % chips] + core) for i in range(chips) for core in (0, 1)
    ]
    back = [(b, a) for a, b in ahead]

    pin = lax.optimization_barrier
    kis, kos = in_proj_up.shape[0], out_proj_up.shape[0]
    seq_count = labels.shape[0]
    pairs, half = seq_count // 2, tokens // 2

    core = (me % 2)[None]

    def send(forward, backward):
        return lax.ppermute(forward, "tensor", ahead), lax.ppermute(backward, "tensor", back)

    f, b = send(out_grad, out_grad)
    other = swap(out_grad, 1, devices)
    own_columns = lax.dynamic_slice_in_dim(out_proj_down, me * depth, depth, axis=1)
    keep, give = first_parts(core, activations, out_grad, in_proj_up, own_columns)
    part = keep + swap(give, 1, devices)
    gate_pre, up_pre, part = pin((gate_pre, up_pre, part))
    silu_gate, a_down = own_parts(gate_pre, up_pre, in_proj_down)
    bits = [1 << i for i in reversed(range(2, devices.bit_length() - 1))]
    rounds = [[]] + [[int(bit) for bit in some] for some in np.array_split(bits, far - 2)]
    row = part.shape[0] // 2
    side = (me // 2) % 2
    give = lax.dynamic_slice_in_dim(part, (1 - side) * row, row, axis=0)
    part = lax.dynamic_slice_in_dim(part, side * row, row, axis=0)

    def ask(part, step):
        return [swap(part.astype(BF16), bit, devices) for bit in rounds[step]]

    def added(part, theirs):
        for more in theirs:
            part = part + more.astype(F32)
        return part

    theirs = [swap(give.astype(BF16), 2, devices)]
    seqs = jnp.arange(seq_count, dtype=jnp.int32)[:, None]
    signs = (2 * labels - 1).astype(F32)
    per_seq = jnp.where(segments[None, :] == seqs, signs[:, None], F32(0.0))
    pair_weight = per_seq.reshape(pairs, 2, tokens).sum(axis=1)

    f, b, theirs, a_down, pair_weight = pin((f, b, theirs, a_down, pair_weight))
    part = added(part, theirs)
    known, came = None, (f, b)
    units = [(out_grad, 0), (other, 1)]
    for step in range(1, far):
        if step < far - 1:
            f, b = send(f, b)
            theirs = ask(part, step)
        else:
            f, b = send(f[:half], b[half:])
        place = 4 * step - 2
        theirs_of = [swap(array, 1, devices) for array in came]
        units += [(array, place + 2 * i) for i, array in enumerate(came)]
        units += [(array, place + 2 * i + 1) for i, array in enumerate(theirs_of)]
        if step == far - 3:
            q_turned = turned(queries, kos)
            src, q_turned = pin((src, q_turned))
        if step == far - 2:
            columns = columns_of(src, down_weight, depth, (devices - 2, devices - 1))
            src, columns = pin((src, columns))
        if step == far - 1:
            quarters = [part] + [swap(part, bit, devices) for bit in (2, 1, 3)]
            known = add_step(src, units, down_weight, known)
            known, quarters = pin((known, quarters))
            high, low, down = pair_parts(
                jnp.stack([me % 2, side]), pair_weight, quarters, a_down
            )
        else:
            known = add_step(src, units, down_weight, known)
            units = []
            f, b, theirs, known = pin((f, b, theirs, known))
            part = added(part, theirs)
            came = (f, b)
    f, b, known = pin((f, b, known))
    halves = [x for block in (f, b) for x in (block, swap(block, 1, devices))]
    up = last_step(halves, columns, silu_gate, out_proj_up, known, (high, low), pairs)

    first = core == 0
    total = jnp.where(first, down, up) + swap(jnp.where(first, up, down), 1, devices)
    for bit in range(1, devices.bit_length() - 1):
        total = total + swap(total.astype(BF16), 1 << bit, devices).astype(F32)
    rest = swap(total, 1, devices)
    return score(jnp.where(first, total, rest), jnp.where(first, rest, total), q_turned)


def solution(mesh):
    in_specs = (
        P("groups", "tensor"),
        P("groups", "tensor"),
        P("groups", "tensor"),
        P("groups", "tensor"),
        P("tensor", None),
        P(None, "tensor"),
        P(),
        P(None, "tensor"),
        P(None, "tensor"),
        P("groups"),
        P("groups"),
        P("tensor", None),
    )
    return jax.shard_map(
        functools.partial(per_device, mesh.shape["tensor"]),
        mesh=mesh,
        in_specs=in_specs,
        out_specs=P("groups", "tensor"),
        check_vma=False,
    )
```

```python
import functools

import jax
import jax.numpy as jnp
import numpy as np
from jax import lax
from jax.experimental import pallas as pl
from jax.experimental.pallas import tpu as pltpu
from jax.sharding import PartitionSpec as P

F32, BF16 = jnp.float32, jnp.bfloat16
VMEM_LIMIT = 24 * 1024 * 1024
SMALL = pl.CostEstimate(flops=1000, bytes_accessed=1000, transcendentals=0)


def dot_t(left, right, precision=None):
    return lax.dot_general(
        left, right, (((1,), (1,)), ((), ())), preferred_element_type=F32, precision=precision
    )


def ring_of(chips):
    if chips == 8:
        return [0, 2, 4, 6, 7, 5, 3, 1]
    return list(range(chips))


def tile_of(units):
    return 256 if units % 256 == 0 else units


def products(lefts, weights):
    total = None
    for i, weight in enumerate(weights):
        part = dot_t(lefts[i], weight[...])
        total = part if total is None else total + part
    return total


def load(blocks, lefts, sems):
    half = lefts.shape[1] // 2
    copies = []
    for i, (array, row) in enumerate(blocks):
        rows = pl.ds((i % 2) * half, half)
        source = array.at[pl.ds(row * half, half)]
        copies.append(pltpu.make_async_copy(source, lefts.at[i // 2, rows], sems.at[i]))
    for copy in copies:
        copy.start()
    for copy in copies:
        copy.wait()


def step_kernel(count, src_ref, *refs):
    blocks, weights = refs[:count], refs[count : 2 * count]
    out_ref, lefts, sems = refs[-3:]
    before_ref = refs[2 * count] if len(refs) == 2 * count + 4 else None
    step = pl.program_id(0)

    @pl.when(step == 0)
    def _():
        load([(block, i) for block in blocks for i in range(2)], lefts, sems)

    total = products(lefts, weights)
    out_ref[step] = total if before_ref is None else total + before_ref[step]


def projected(ups, proj_ref):
    total, tile = None, ups.shape[2]
    for i in range(ups.shape[0]):
        part = dot_t(ups[i], proj_ref[:, i * tile : (i + 1) * tile])
        total = part if total is None else total + part
    return total


def in_hbm(x):
    return pltpu.with_memory_space_constraint(x, pltpu.HBM)


def in_vmem(x):
    return pltpu.with_memory_space_constraint(x, pltpu.VMEM)


ANYWHERE = pl.BlockSpec(memory_space=pl.ANY)
WHOLE = pl.BlockSpec(memory_space=pltpu.VMEM)


def step_parts(units, weight):
    tokens, depth = units[0][0].shape
    tile = tile_of(weight.shape[0])
    ins = [in_hbm(array) if place == 0 else array for array, place in units]
    ins += [in_hbm(weight)] * len(units)
    specs = [ANYWHERE] * len(units)
    specs += [pl.BlockSpec((tile, depth), lambda i, s, m=m: (i, s[m])) for _, m in units]
    scratch = [
        pltpu.VMEM((len(units), tokens, depth), BF16),
        pltpu.SemaphoreType.DMA((2 * len(units),)),
    ]
    return ins, specs, scratch, tile


def add_step(src, units, weight, before):
    ins, specs, scratch, tile = step_parts(units, weight)
    tokens, hidden = units[0][0].shape[0], weight.shape[0]
    aliases = {}
    if before is not None:
        ins.append(in_vmem(before))
        specs.append(WHOLE)
        aliases = {len(ins): 0}
    return pl.pallas_call(
        functools.partial(step_kernel, len(units)),
        grid_spec=pltpu.PrefetchScalarGridSpec(
            num_scalar_prefetch=1,
            grid=(hidden // tile,),
            in_specs=specs,
            out_specs=WHOLE,
            scratch_shapes=scratch,
        ),
        out_shape=pltpu.VMEM((hidden // tile, tokens, tile), F32),
        input_output_aliases=aliases,
        cost_estimate=SMALL,
        compiler_params=pltpu.CompilerParams(vmem_limit_bytes=VMEM_LIMIT),
    )(src, *ins)


def columns_kernel(places, src_ref, weight_ref, out_ref, sems):
    depth = out_ref.shape[2]
    copies = []
    for i, place in enumerate(places):
        start = pl.multiple_of(src_ref[place] * depth, depth)
        copies.append(
            pltpu.make_async_copy(weight_ref.at[:, pl.ds(start, depth)], out_ref.at[i], sems.at[i])
        )
    for copy in copies:
        copy.start()
    for copy in copies:
        copy.wait()


def columns_of(src, weight, depth, places):
    return pl.pallas_call(
        functools.partial(columns_kernel, places),
        grid_spec=pltpu.PrefetchScalarGridSpec(
            num_scalar_prefetch=1,
            grid=(),
            in_specs=[ANYWHERE],
            out_specs=WHOLE,
            scratch_shapes=[pltpu.SemaphoreType.DMA((len(places),))],
        ),
        out_shape=pltpu.VMEM((len(places), weight.shape[0], depth), BF16),
        cost_estimate=SMALL,
        compiler_params=pltpu.CompilerParams(vmem_limit_bytes=VMEM_LIMIT),
    )(src, in_hbm(weight))


def last_kernel(*refs):
    halves = refs[:4]
    weight_ref, silu_ref, proj_ref, before_ref, high_ref, low_ref, out_ref, lefts, ups, sems = refs[4:]
    half, tile = lefts.shape[1] // 2, ups.shape[2]
    load([(halves[i], 0) for i in (0, 2, 1, 3)], lefts, sems)
    for i in range(ups.shape[0]):
        cols = slice(i * tile, (i + 1) * tile)
        for h in range(2):
            rows = slice(h * half, (h + 1) * half)
            grad = before_ref[i, rows, :]
            for m in range(lefts.shape[0]):
                grad = grad + dot_t(lefts[m, rows, :], weight_ref[m, cols, :])
            ups[i, rows, :] = (grad * silu_ref[i, rows, :]).astype(BF16)
    b_high, b_low = parts_of(projected(ups, proj_ref))
    kos = b_high.shape[1]
    sums = jnp.dot(
        high_ref[...], jnp.concatenate([b_high, b_low], axis=1), preferred_element_type=F32
    )
    rest = jnp.dot(low_ref[...], b_high, preferred_element_type=F32)
    out_ref[...] = spread(sums[:, :kos] + (sums[:, kos:] + rest), out_ref.shape[0])


def last_step(halves, columns, silu, proj_up, before, up, pairs):
    tiles, tokens, tile = silu.shape
    depth, kos = halves[0].shape[1], proj_up.shape[0]
    ins = [in_vmem(x) for x in (columns, silu, proj_up, before, *up)]
    return pl.pallas_call(
        last_kernel,
        in_specs=[ANYWHERE] * 4 + [WHOLE] * len(ins),
        out_specs=WHOLE,
        out_shape=jax.ShapeDtypeStruct((pairs, up[0].shape[0] // pairs * kos), F32),
        scratch_shapes=[
            pltpu.VMEM((2, tokens, depth), BF16),
            pltpu.VMEM((tiles, tokens, tile), BF16),
            pltpu.SemaphoreType.DMA((4,)),
        ],
        cost_estimate=SMALL,
        compiler_params=pltpu.CompilerParams(vmem_limit_bytes=VMEM_LIMIT),
    )(*halves, *ins)


def own_kernel(gate_ref, up_ref, down_ref, silu_ref, out_ref, hidden):
    step, tile = pl.program_id(0), gate_ref.shape[1]
    gate = gate_ref[...].astype(F32)
    silu = gate / (1.0 + jnp.exp(-gate))
    silu_ref[step] = silu
    hidden[step] = (silu * up_ref[...].astype(F32)).astype(BF16)

    @pl.when(step == hidden.shape[0] - 1)
    def _():
        total = None
        for i in range(hidden.shape[0]):
            part = dot_t(down_ref[:, i * tile : (i + 1) * tile], hidden[i])
            total = part if total is None else total + part
        out_ref[...] = total


def own_parts(gate, up, in_down):
    tokens, units = gate.shape
    tile, kis = tile_of(units), in_down.shape[0]
    tiles = pl.BlockSpec((tokens, tile), lambda i: (0, i))
    return pl.pallas_call(
        own_kernel,
        grid=(units // tile,),
        in_specs=[tiles, tiles, pl.BlockSpec((kis, units), lambda i: (0, 0))],
        out_specs=(WHOLE, pl.BlockSpec((kis, tokens), lambda i: (0, 0))),
        out_shape=(
            pltpu.VMEM((units // tile, tokens, tile), F32),
            jax.ShapeDtypeStruct((kis, tokens), F32),
        ),
        scratch_shapes=[pltpu.VMEM((units // tile, tokens, tile), BF16)],
        cost_estimate=SMALL,
        compiler_params=pltpu.CompilerParams(vmem_limit_bytes=VMEM_LIMIT),
    )(in_hbm(gate), in_hbm(up), in_down)


def turned(q, kos):
    asked, size = q.shape[0], q.shape[1] // 2
    kis = size // kos

    def kernel(q_ref, out_ref, rows):
        rows[...] = q_ref[...].astype(F32).T
        for j in range(kis):
            out_ref[j * kos : (j + 1) * kos, :] = rows[pl.ds(j, kos, stride=kis), :].astype(BF16)

    return pl.pallas_call(
        kernel,
        grid=(2,),
        in_specs=[pl.BlockSpec((asked, size), lambda i: (0, i))],
        out_specs=pl.BlockSpec((size, asked), lambda i: (i, 0)),
        out_shape=jax.ShapeDtypeStruct((2 * size, asked), BF16),
        scratch_shapes=[pltpu.VMEM((size, asked), F32)],
        cost_estimate=SMALL,
        compiler_params=pltpu.CompilerParams(vmem_limit_bytes=VMEM_LIMIT),
    )(in_hbm(q))


def score_kernel(down_ref, up_ref, q_ref, out_ref):
    pairs, size = down_ref.shape
    total = None
    for i, ref in enumerate((down_ref, up_ref)):
        both = jnp.concatenate(parts_of(ref[...]), axis=0)
        part = jnp.dot(both, q_ref[i * size : (i + 1) * size, :], preferred_element_type=F32)
        total = part if total is None else total + part
    out_ref[...] = total[:pairs] + total[pairs:]


def score(down, up, q):
    return pl.pallas_call(
        score_kernel,
        out_shape=jax.ShapeDtypeStruct((down.shape[0], q.shape[1]), F32),
        cost_estimate=SMALL,
        compiler_params=pltpu.CompilerParams(vmem_limit_bytes=VMEM_LIMIT),
    )(down, up, q)


def parts_of(x):
    high = x.astype(BF16)
    return high, (x - high.astype(F32)).astype(BF16)


def weighted(weight, a):
    return parts_of(jnp.concatenate([weight * a[j : j + 1, :] for j in range(a.shape[0])], axis=0))


def spread(sums, pairs):
    return jnp.concatenate([sums[r : r + pairs] for r in range(0, sums.shape[0], pairs)], axis=1)


def first_kernel(core_ref, acts_ref, grad_ref, in_up_ref, columns_ref, keep_ref, give_ref):
    first = core_ref[0] == 0
    a, b = dot_t(in_up_ref[...], acts_ref[...]), dot_t(columns_ref[...], grad_ref[...])
    half = a.shape[0] // 2
    for rows, x in ((slice(0, half), a), (slice(half, 2 * half), b)):
        keep_ref[rows, :] = jnp.where(first, x[:half], x[half:])
        give_ref[rows, :] = jnp.where(first, x[half:], x[:half])


def first_parts(core, acts, grad, in_up, columns):
    shape = jax.ShapeDtypeStruct((in_up.shape[0], acts.shape[0]), F32)
    whole = pl.BlockSpec(memory_space=pltpu.VMEM)
    return pl.pallas_call(
        first_kernel,
        in_specs=[pl.BlockSpec(memory_space=pltpu.SMEM)] + [whole] * 4,
        out_specs=(whole, whole),
        out_shape=(shape, shape),
        cost_estimate=SMALL,
        compiler_params=pltpu.CompilerParams(vmem_limit_bytes=VMEM_LIMIT),
    )(core, acts, grad, in_up, columns)


def pair_kernel(place_ref, weight_ref, mine_ref, across_ref, mine1_ref, across1_ref, a_ref, high_ref, low_ref, out_ref):
    first, near = place_ref[0] == 0, place_ref[1] == 0
    rows = []
    for mine, across in ((mine_ref, across_ref), (mine1_ref, across1_ref)):
        mine, across = mine[...], across[...].astype(F32)
        rows.append((jnp.where(near, mine, across), jnp.where(near, across, mine)))
    (a0, b0), (a1, b1) = rows
    a_up = jnp.concatenate([jnp.where(first, a0, a1), jnp.where(first, a1, a0)], axis=0)
    b_down = jnp.concatenate([jnp.where(first, b0, b1), jnp.where(first, b1, b0)], axis=0)
    weight = weight_ref[...]
    high_ref[...], low_ref[...] = weighted(weight, a_up)
    b_high, b_low = parts_of(b_down)
    high, low = weighted(weight, a_ref[...])
    sums = dot_t(high, b_high) + (dot_t(high, b_low) + dot_t(low, b_high))
    out_ref[...] = spread(sums, weight.shape[0])


def pair_parts(place, weight, quarters, a_down):
    pairs, tokens = weight.shape
    kis, kos = a_down.shape[0], 2 * quarters[0].shape[0]
    shape = pltpu.VMEM((pairs * kis, tokens), BF16)
    return pl.pallas_call(
        pair_kernel,
        in_specs=[pl.BlockSpec(memory_space=pltpu.SMEM)] + [WHOLE] * 6,
        out_specs=(WHOLE, WHOLE, WHOLE),
        out_shape=(shape, shape, jax.ShapeDtypeStruct((pairs, kis * kos), F32)),
        cost_estimate=SMALL,
        compiler_params=pltpu.CompilerParams(vmem_limit_bytes=VMEM_LIMIT),
    )(place, weight, *quarters, a_down)


def swap(value, bit, devices):
    return lax.ppermute(value, "tensor", [(i, i ^ bit) for i in range(devices)])


def per_device(
    devices,
    activations,
    gate_pre,
    up_pre,
    out_grad,
    down_weight,
    in_proj_down,
    out_proj_down,
    in_proj_up,
    out_proj_up,
    segments,
    labels,
    queries,
):
    tokens, depth = out_grad.shape
    me = lax.axis_index("tensor")
    chips = devices // 2
    ring = ring_of(chips)
    far = chips // 2
    place = {chip: i for i, chip in enumerate(ring)}

    table = np.zeros((devices, devices), np.int32)
    for device in range(devices):
        chip, core = divmod(device, 2)
        order = [chip]
        for step in range(1, far):
            order += [ring[(place[chip] - step) % chips], ring[(place[chip] + step) % chips]]
        order.append(ring[(place[chip] + far) % chips])
        table[device] = [2 * c + k for c in order for k in (core, 1 - core)]
    src = lax.dynamic_index_in_dim(jnp.asarray(table), me, 0, keepdims=False)

    ahead = [
        (2 * ring[i] + core, 2 * ring[(i + 1) % chips] + core) for i in range(chips) for core in (0, 1)
    ]
    back = [(b, a) for a, b in ahead]

    pin = lax.optimization_barrier
    kis, kos = in_proj_up.shape[0], out_proj_up.shape[0]
    seq_count = labels.shape[0]
    pairs, half = seq_count // 2, tokens // 2

    core = (me % 2)[None]

    def send(forward, backward):
        return lax.ppermute(forward, "tensor", ahead), lax.ppermute(backward, "tensor", back)

    f, b = send(out_grad, out_grad)
    other = swap(out_grad, 1, devices)
    own_columns = lax.dynamic_slice_in_dim(out_proj_down, me * depth, depth, axis=1)
    keep, give = first_parts(core, activations, out_grad, in_proj_up, own_columns)
    part = keep + swap(give, 1, devices)
    gate_pre, up_pre, part = pin((gate_pre, up_pre, part))
    silu_gate, a_down = own_parts(gate_pre, up_pre, in_proj_down)
    bits = [1 << i for i in reversed(range(2, devices.bit_length() - 1))]
    rounds = [[]] + [[int(bit) for bit in some] for some in np.array_split(bits, far - 2)]
    row = part.shape[0] // 2
    side = (me // 2) % 2
    give = lax.dynamic_slice_in_dim(part, (1 - side) * row, row, axis=0)
    part = lax.dynamic_slice_in_dim(part, side * row, row, axis=0)

    def ask(part, step):
        return [swap(part.astype(BF16), bit, devices) for bit in rounds[step]]

    def added(part, theirs):
        for more in theirs:
            part = part + more.astype(F32)
        return part

    theirs = [swap(give.astype(BF16), 2, devices)]
    seqs = jnp.arange(seq_count, dtype=jnp.int32)[:, None]
    signs = (2 * labels - 1).astype(F32)
    per_seq = jnp.where(segments[None, :] == seqs, signs[:, None], F32(0.0))
    pair_weight = per_seq.reshape(pairs, 2, tokens).sum(axis=1)

    f, b, theirs, a_down, pair_weight = pin((f, b, theirs, a_down, pair_weight))
    part = added(part, theirs)
    known, came = None, (f, b)
    units = [(out_grad, 0), (other, 1)]
    for step in range(1, far):
        if step < far - 1:
            f, b = send(f, b)
            theirs = ask(part, step)
        else:
            f, b = send(f[:half], b[half:])
        place = 4 * step - 2
        theirs_of = [swap(array, 1, devices) for array in came]
        units += [(array, place + 2 * i) for i, array in enumerate(came)]
        units += [(array, place + 2 * i + 1) for i, array in enumerate(theirs_of)]
        if step == far - 2:
            q_turned = turned(queries, kos)
            columns = columns_of(src, down_weight, depth, (devices - 2, devices - 1))
            src, columns, q_turned = pin((src, columns, q_turned))
        if step == far - 1:
            near = [part, swap(part, 1, devices)]
            beyond = [swap(part.astype(BF16), bit, devices) for bit in (2, 3)]
            quarters = [near[0], beyond[0], near[1], beyond[1]]
            known = add_step(src, units, down_weight, known)
            known, quarters = pin((known, quarters))
            high, low, down = pair_parts(
                jnp.stack([me % 2, side]), pair_weight, quarters, a_down
            )
        else:
            known = add_step(src, units, down_weight, known)
            units = []
            f, b, theirs, known = pin((f, b, theirs, known))
            part = added(part, theirs)
            came = (f, b)
    f, b, known = pin((f, b, known))
    halves = [x for block in (f, b) for x in (block, swap(block, 1, devices))]
    up = last_step(halves, columns, silu_gate, out_proj_up, known, (high, low), pairs)

    first = core == 0
    total = jnp.where(first, down, up) + swap(jnp.where(first, up, down), 1, devices)
    for bit in range(1, devices.bit_length() - 1):
        total = total + swap(total.astype(BF16), 1 << bit, devices).astype(F32)
    rest = swap(total, 1, devices)
    return score(jnp.where(first, total, rest), jnp.where(first, rest, total), q_turned)


def solution(mesh):
    in_specs = (
        P("groups", "tensor"),
        P("groups", "tensor"),
        P("groups", "tensor"),
        P("groups", "tensor"),
        P("tensor", None),
        P(None, "tensor"),
        P(),
        P(None, "tensor"),
        P(None, "tensor"),
        P("groups"),
        P("groups"),
        P("tensor", None),
    )
    return jax.shard_map(
        functools.partial(per_device, mesh.shape["tensor"]),
        mesh=mesh,
        in_specs=in_specs,
        out_specs=P("groups", "tensor"),
        check_vma=False,
    )
```

```python
import functools

import jax
import jax.numpy as jnp
import numpy as np
from jax import lax
from jax.experimental import pallas as pl
from jax.experimental.pallas import tpu as pltpu
from jax.sharding import PartitionSpec as P

F32, BF16 = jnp.float32, jnp.bfloat16
VMEM_LIMIT = 14 * 1024 * 1024
SMALL = pl.CostEstimate(flops=1000, bytes_accessed=1000, transcendentals=0)


def dot_t(left, right, precision=None):
    return lax.dot_general(
        left, right, (((1,), (1,)), ((), ())), preferred_element_type=F32, precision=precision
    )


def ring_of(chips):
    if chips == 8:
        return [0, 2, 4, 6, 7, 5, 3, 1]
    return list(range(chips))


def tile_of(units):
    return 256 if units % 256 == 0 else units


def products(lefts, weights):
    total = None
    for i, weight in enumerate(weights):
        part = dot_t(lefts[i][...], weight[...])
        total = part if total is None else total + part
    return total


def load(blocks, lefts, sems):
    half = lefts.shape[1] // 2
    copies = []
    for i, (array, row) in enumerate(blocks):
        rows = pl.ds((i % 2) * half, half)
        source = array.at[pl.ds(row * half, half)]
        copies.append(pltpu.make_async_copy(source, lefts.at[i // 2, rows], sems.at[i]))
    for copy in copies:
        copy.start()
    for copy in copies:
        copy.wait()


def step_kernel(count, src_ref, *refs):
    blocks, weights = refs[:count], refs[count : 2 * count]
    out_ref, lefts, sems = refs[-3:]
    before_ref = refs[2 * count] if len(refs) == 2 * count + 4 else None
    step = pl.program_id(0)

    @pl.when(step == 0)
    def _():
        load([(block, i) for block in blocks for i in range(2)], lefts, sems)

    total = products(lefts, weights)
    out_ref[step] = total if before_ref is None else total + before_ref[step]


def near_kernel(*refs):
    blocks, weight_ref, before_ref, out_ref = refs[:4], refs[4], refs[5], refs[6]
    tiles, _, tile = out_ref.shape
    for i in range(tiles):
        cols = slice(i * tile, (i + 1) * tile)
        total = before_ref[i]
        for m, block in enumerate(blocks):
            total = total + dot_t(block[...], weight_ref[m, cols, :])
        out_ref[i] = total


def near_step(blocks, columns, before):
    ins = [in_vmem(x) for x in (*blocks, columns, before)]
    return pl.pallas_call(
        near_kernel,
        in_specs=[WHOLE] * len(ins),
        out_specs=WHOLE,
        out_shape=pltpu.VMEM(before.shape, F32),
        input_output_aliases={len(ins) - 1: 0},
        cost_estimate=SMALL,
        compiler_params=pltpu.CompilerParams(vmem_limit_bytes=VMEM_LIMIT),
    )(*ins)


def projected(ups, proj_ref):
    total, tile = None, ups.shape[2]
    for i in range(ups.shape[0]):
        part = dot_t(ups[i], proj_ref[:, i * tile : (i + 1) * tile])
        total = part if total is None else total + part
    return total


def in_hbm(x):
    return pltpu.with_memory_space_constraint(x, pltpu.HBM)


def in_vmem(x):
    return pltpu.with_memory_space_constraint(x, pltpu.VMEM)


ANYWHERE = pl.BlockSpec(memory_space=pl.ANY)
WHOLE = pl.BlockSpec(memory_space=pltpu.VMEM)


def step_parts(units, weight):
    tokens, depth = units[0][0].shape
    tile = tile_of(weight.shape[0])
    ins = [in_hbm(array) if place == 0 else array for array, place in units]
    ins += [in_hbm(weight)] * len(units)
    specs = [ANYWHERE] * len(units)
    specs += [pl.BlockSpec((tile, depth), lambda i, s, m=m: (i, s[m])) for _, m in units]
    scratch = [
        pltpu.VMEM((len(units), tokens, depth), BF16),
        pltpu.SemaphoreType.DMA((2 * len(units),)),
    ]
    return ins, specs, scratch, tile


def add_step(src, units, weight, before):
    ins, specs, scratch, tile = step_parts(units, weight)
    tokens, hidden = units[0][0].shape[0], weight.shape[0]
    aliases = {}
    if before is not None:
        ins.append(in_vmem(before))
        specs.append(WHOLE)
        aliases = {len(ins): 0}
    return pl.pallas_call(
        functools.partial(step_kernel, len(units)),
        grid_spec=pltpu.PrefetchScalarGridSpec(
            num_scalar_prefetch=1,
            grid=(hidden // tile,),
            in_specs=specs,
            out_specs=WHOLE,
            scratch_shapes=scratch,
        ),
        out_shape=pltpu.VMEM((hidden // tile, tokens, tile), F32),
        input_output_aliases=aliases,
        cost_estimate=SMALL,
        compiler_params=pltpu.CompilerParams(vmem_limit_bytes=VMEM_LIMIT),
    )(src, *ins)


def columns_kernel(places, src_ref, weight_ref, out_ref, sems):
    depth = out_ref.shape[2]
    copies = []
    for i, place in enumerate(places):
        start = pl.multiple_of(src_ref[place] * depth, depth)
        copies.append(
            pltpu.make_async_copy(weight_ref.at[:, pl.ds(start, depth)], out_ref.at[i], sems.at[i])
        )
    for copy in copies:
        copy.start()
    for copy in copies:
        copy.wait()


def columns_of(src, weight, depth, places):
    return pl.pallas_call(
        functools.partial(columns_kernel, places),
        grid_spec=pltpu.PrefetchScalarGridSpec(
            num_scalar_prefetch=1,
            grid=(),
            in_specs=[ANYWHERE],
            out_specs=WHOLE,
            scratch_shapes=[pltpu.SemaphoreType.DMA((len(places),))],
        ),
        out_shape=pltpu.VMEM((len(places), weight.shape[0], depth), BF16),
        cost_estimate=SMALL,
        compiler_params=pltpu.CompilerParams(vmem_limit_bytes=VMEM_LIMIT),
    )(src, in_hbm(weight))


def last_kernel(*refs):
    halves = refs[:4]
    weight_ref, silu_ref, proj_ref, before_ref, high_ref, low_ref, out_ref, ups = refs[4:]
    half, tile = halves[0].shape[0], ups.shape[2]
    for i in range(ups.shape[0]):
        cols = slice(i * tile, (i + 1) * tile)
        for h in range(2):
            rows = slice(h * half, (h + 1) * half)
            grad = before_ref[i, rows, :]
            for m in range(2):
                grad = grad + dot_t(halves[2 * h + m][...], weight_ref[m, cols, :])
            ups[i, rows, :] = (grad * silu_ref[i, rows, :]).astype(BF16)
    b_high, b_low = parts_of(projected(ups, proj_ref))
    kos = b_high.shape[1]
    sums = jnp.dot(
        high_ref[...], jnp.concatenate([b_high, b_low], axis=1), preferred_element_type=F32
    )
    rest = jnp.dot(low_ref[...], b_high, preferred_element_type=F32)
    out_ref[...] = spread(sums[:, :kos] + (sums[:, kos:] + rest), out_ref.shape[0])


def last_step(halves, columns, silu, proj_up, before, up, pairs):
    tiles, tokens, tile = silu.shape
    kos = proj_up.shape[0]
    ins = [in_vmem(x) for x in (*halves, columns, silu, proj_up, before, *up)]
    return pl.pallas_call(
        last_kernel,
        in_specs=[WHOLE] * len(ins),
        out_specs=WHOLE,
        out_shape=jax.ShapeDtypeStruct((pairs, up[0].shape[0] // pairs * kos), F32),
        scratch_shapes=[pltpu.VMEM((tiles, tokens, tile), BF16)],
        cost_estimate=SMALL,
        compiler_params=pltpu.CompilerParams(vmem_limit_bytes=VMEM_LIMIT),
    )(*ins)


def own_kernel(gate_ref, up_ref, down_ref, silu_ref, out_ref, hidden):
    step, tile = pl.program_id(0), gate_ref.shape[1]
    gate = gate_ref[...].astype(F32)
    silu = gate / (1.0 + jnp.exp(-gate))
    silu_ref[step] = silu
    hidden[step] = (silu * up_ref[...].astype(F32)).astype(BF16)

    @pl.when(step == hidden.shape[0] - 1)
    def _():
        total = None
        for i in range(hidden.shape[0]):
            part = dot_t(down_ref[:, i * tile : (i + 1) * tile], hidden[i])
            total = part if total is None else total + part
        out_ref[...] = total


def own_parts(gate, up, in_down):
    tokens, units = gate.shape
    tile, kis = tile_of(units), in_down.shape[0]
    tiles = pl.BlockSpec((tokens, tile), lambda i: (0, i))
    return pl.pallas_call(
        own_kernel,
        grid=(units // tile,),
        in_specs=[tiles, tiles, pl.BlockSpec((kis, units), lambda i: (0, 0))],
        out_specs=(WHOLE, pl.BlockSpec((kis, tokens), lambda i: (0, 0))),
        out_shape=(
            pltpu.VMEM((units // tile, tokens, tile), F32),
            jax.ShapeDtypeStruct((kis, tokens), F32),
        ),
        scratch_shapes=[pltpu.VMEM((units // tile, tokens, tile), BF16)],
        cost_estimate=SMALL,
        compiler_params=pltpu.CompilerParams(vmem_limit_bytes=VMEM_LIMIT),
    )(in_hbm(gate), in_hbm(up), in_down)


def turned(q, kos):
    asked, size = q.shape[0], q.shape[1] // 2
    kis = size // kos

    def kernel(q_ref, out_ref, rows):
        rows[...] = q_ref[...].astype(F32).T
        for j in range(kis):
            out_ref[j * kos : (j + 1) * kos, :] = rows[pl.ds(j, kos, stride=kis), :].astype(BF16)

    return pl.pallas_call(
        kernel,
        grid=(2,),
        in_specs=[pl.BlockSpec((asked, size), lambda i: (0, i))],
        out_specs=pl.BlockSpec((size, asked), lambda i: (i, 0)),
        out_shape=jax.ShapeDtypeStruct((2 * size, asked), BF16),
        scratch_shapes=[pltpu.VMEM((size, asked), F32)],
        cost_estimate=SMALL,
        compiler_params=pltpu.CompilerParams(vmem_limit_bytes=VMEM_LIMIT),
    )(in_hbm(q))


def score_kernel(down_ref, up_ref, q_ref, out_ref):
    pairs, size = down_ref.shape
    total = None
    for i, ref in enumerate((down_ref, up_ref)):
        both = jnp.concatenate(parts_of(ref[...]), axis=0)
        part = jnp.dot(both, q_ref[i * size : (i + 1) * size, :], preferred_element_type=F32)
        total = part if total is None else total + part
    out_ref[...] = total[:pairs] + total[pairs:]


def score(down, up, q):
    return pl.pallas_call(
        score_kernel,
        out_shape=jax.ShapeDtypeStruct((down.shape[0], q.shape[1]), F32),
        cost_estimate=SMALL,
        compiler_params=pltpu.CompilerParams(vmem_limit_bytes=VMEM_LIMIT),
    )(down, up, q)


def parts_of(x):
    high = x.astype(BF16)
    return high, (x - high.astype(F32)).astype(BF16)


def weighted(weight, a):
    return parts_of(jnp.concatenate([weight * a[j : j + 1, :] for j in range(a.shape[0])], axis=0))


def spread(sums, pairs):
    return jnp.concatenate([sums[r : r + pairs] for r in range(0, sums.shape[0], pairs)], axis=1)


def first_kernel(core_ref, acts_ref, grad_ref, in_up_ref, columns_ref, keep_ref, give_ref):
    first = core_ref[0] == 0
    a, b = dot_t(in_up_ref[...], acts_ref[...]), dot_t(columns_ref[...], grad_ref[...])
    half = a.shape[0] // 2
    for rows, x in ((slice(0, half), a), (slice(half, 2 * half), b)):
        keep_ref[rows, :] = jnp.where(first, x[:half], x[half:])
        give_ref[rows, :] = jnp.where(first, x[half:], x[:half])


def first_parts(core, acts, grad, in_up, columns):
    shape = jax.ShapeDtypeStruct((in_up.shape[0], acts.shape[0]), F32)
    whole = pl.BlockSpec(memory_space=pltpu.VMEM)
    return pl.pallas_call(
        first_kernel,
        in_specs=[pl.BlockSpec(memory_space=pltpu.SMEM)] + [whole] * 4,
        out_specs=(whole, whole),
        out_shape=(shape, shape),
        cost_estimate=SMALL,
        compiler_params=pltpu.CompilerParams(vmem_limit_bytes=VMEM_LIMIT),
    )(core, acts, grad, in_up, columns)


def pair_kernel(place_ref, weight_ref, mine_ref, across_ref, mine1_ref, across1_ref, a_ref, high_ref, low_ref, out_ref):
    first, near = place_ref[0] == 0, place_ref[1] == 0
    rows = []
    for mine, across in ((mine_ref, across_ref), (mine1_ref, across1_ref)):
        mine, across = mine[...], across[...].astype(F32)
        rows.append((jnp.where(near, mine, across), jnp.where(near, across, mine)))
    (a0, b0), (a1, b1) = rows
    a_up = jnp.concatenate([jnp.where(first, a0, a1), jnp.where(first, a1, a0)], axis=0)
    b_down = jnp.concatenate([jnp.where(first, b0, b1), jnp.where(first, b1, b0)], axis=0)
    weight = weight_ref[...]
    high_ref[...], low_ref[...] = weighted(weight, a_up)
    b_high, b_low = parts_of(b_down)
    high, low = weighted(weight, a_ref[...])
    sums = dot_t(high, b_high) + (dot_t(high, b_low) + dot_t(low, b_high))
    out_ref[...] = spread(sums, weight.shape[0])


def pair_parts(place, weight, quarters, a_down):
    pairs, tokens = weight.shape
    kis, kos = a_down.shape[0], 2 * quarters[0].shape[0]
    shape = pltpu.VMEM((pairs * kis, tokens), BF16)
    return pl.pallas_call(
        pair_kernel,
        in_specs=[pl.BlockSpec(memory_space=pltpu.SMEM)] + [WHOLE] * 6,
        out_specs=(WHOLE, WHOLE, WHOLE),
        out_shape=(shape, shape, jax.ShapeDtypeStruct((pairs, kis * kos), F32)),
        cost_estimate=SMALL,
        compiler_params=pltpu.CompilerParams(vmem_limit_bytes=VMEM_LIMIT),
    )(place, weight, *quarters, a_down)


def swap(value, bit, devices):
    return lax.ppermute(value, "tensor", [(i, i ^ bit) for i in range(devices)])


def per_device(
    devices,
    activations,
    gate_pre,
    up_pre,
    out_grad,
    down_weight,
    in_proj_down,
    out_proj_down,
    in_proj_up,
    out_proj_up,
    segments,
    labels,
    queries,
):
    tokens, depth = out_grad.shape
    me = lax.axis_index("tensor")
    chips = devices // 2
    ring = ring_of(chips)
    far = chips // 2
    place = {chip: i for i, chip in enumerate(ring)}

    table = np.zeros((devices, devices), np.int32)
    for device in range(devices):
        chip, core = divmod(device, 2)
        order = [chip]
        for step in range(1, far):
            order += [ring[(place[chip] - step) % chips], ring[(place[chip] + step) % chips]]
        order.append(ring[(place[chip] + far) % chips])
        table[device] = [2 * c + k for c in order for k in (core, 1 - core)]
    src = lax.dynamic_index_in_dim(jnp.asarray(table), me, 0, keepdims=False)

    ahead = [
        (2 * ring[i] + core, 2 * ring[(i + 1) % chips] + core) for i in range(chips) for core in (0, 1)
    ]
    back = [(b, a) for a, b in ahead]

    pin = lax.optimization_barrier
    kis, kos = in_proj_up.shape[0], out_proj_up.shape[0]
    seq_count = labels.shape[0]
    pairs, half = seq_count // 2, tokens // 2

    core = (me % 2)[None]

    def send(forward, backward):
        return lax.ppermute(forward, "tensor", ahead), lax.ppermute(backward, "tensor", back)

    f, b = send(out_grad, out_grad)
    other = swap(out_grad, 1, devices)
    own_columns = lax.dynamic_slice_in_dim(out_proj_down, me * depth, depth, axis=1)
    keep, give = first_parts(core, activations, out_grad, in_proj_up, own_columns)
    part = keep + swap(give, 1, devices)
    gate_pre, up_pre, part = pin((gate_pre, up_pre, part))
    silu_gate, a_down = own_parts(gate_pre, up_pre, in_proj_down)
    bits = [1 << i for i in reversed(range(2, devices.bit_length() - 1))]
    rounds = [[]] + [[int(bit) for bit in some] for some in np.array_split(bits, far - 2)]
    row = part.shape[0] // 2
    side = (me // 2) % 2
    give = lax.dynamic_slice_in_dim(part, (1 - side) * row, row, axis=0)
    part = lax.dynamic_slice_in_dim(part, side * row, row, axis=0)

    def ask(part, step):
        return [swap(part.astype(BF16), bit, devices) for bit in rounds[step]]

    def added(part, theirs):
        for more in theirs:
            part = part + more.astype(F32)
        return part

    theirs = [swap(give.astype(BF16), 2, devices)]
    seqs = jnp.arange(seq_count, dtype=jnp.int32)[:, None]
    signs = (2 * labels - 1).astype(F32)
    per_seq = jnp.where(segments[None, :] == seqs, signs[:, None], F32(0.0))
    pair_weight = per_seq.reshape(pairs, 2, tokens).sum(axis=1)

    f, b, theirs, a_down, pair_weight = pin((f, b, theirs, a_down, pair_weight))
    part = added(part, theirs)
    known, came = None, (f, b)
    units = [(out_grad, 0), (other, 1)]
    for step in range(1, far):
        if step < far - 1:
            f, b = send(f, b)
            theirs = ask(part, step)
        else:
            f, b = send(f[:half], b[half:])
        place = 4 * step - 2
        theirs_of = [swap(array, 1, devices) for array in came]
        units += [(array, place + 2 * i) for i, array in enumerate(came)]
        units += [(array, place + 2 * i + 1) for i, array in enumerate(theirs_of)]
        if step == far - 2:
            q_turned = turned(queries, kos)
            columns = [
                columns_of(src, down_weight, depth, places)
                for places in ([place + i for i in (4, 6, 5, 7)], [devices - 2, devices - 1])
            ]
            src, columns, q_turned = pin((src, columns, q_turned))
        if step == far - 1:
            near = [part, swap(part, 1, devices)]
            beyond = [swap(part.astype(BF16), bit, devices) for bit in (2, 3)]
            quarters = [near[0], beyond[0], near[1], beyond[1]]
            known = near_step([array for array, _ in units], columns[0], known)
            known, quarters = pin((known, quarters))
            high, low, down = pair_parts(
                jnp.stack([me % 2, side]), pair_weight, quarters, a_down
            )
        else:
            known = add_step(src, units, down_weight, known)
            units = []
            f, b, theirs, known = pin((f, b, theirs, known))
            part = added(part, theirs)
            came = (f, b)
    f, b, known = pin((f, b, known))
    halves = [x for block in (f, b) for x in (block, swap(block, 1, devices))]
    up = last_step(halves, columns[1], silu_gate, out_proj_up, known, (high, low), pairs)

    first = core == 0
    total = jnp.where(first, down, up) + swap(jnp.where(first, up, down), 1, devices)
    for bit in range(1, devices.bit_length() - 1):
        total = total + swap(total.astype(BF16), 1 << bit, devices).astype(F32)
    rest = swap(total, 1, devices)
    return score(jnp.where(first, total, rest), jnp.where(first, rest, total), q_turned)


def solution(mesh):
    in_specs = (
        P("groups", "tensor"),
        P("groups", "tensor"),
        P("groups", "tensor"),
        P("groups", "tensor"),
        P("tensor", None),
        P(None, "tensor"),
        P(),
        P(None, "tensor"),
        P(None, "tensor"),
        P("groups"),
        P("groups"),
        P("tensor", None),
    )
    return jax.shard_map(
        functools.partial(per_device, mesh.shape["tensor"]),
        mesh=mesh,
        in_specs=in_specs,
        out_specs=P("groups", "tensor"),
        check_vma=False,
    )
```

```python
import functools

import jax
import jax.numpy as jnp
import numpy as np
from jax import lax
from jax.experimental import pallas as pl
from jax.experimental.pallas import tpu as pltpu
from jax.sharding import PartitionSpec as P

F32, BF16 = jnp.float32, jnp.bfloat16
VMEM_LIMIT = 14 * 1024 * 1024
SMALL = pl.CostEstimate(flops=1000, bytes_accessed=1000, transcendentals=0)


def dot_t(left, right, precision=None):
    return lax.dot_general(
        left, right, (((1,), (1,)), ((), ())), preferred_element_type=F32, precision=precision
    )


def ring_of(chips):
    if chips == 8:
        return [0, 2, 4, 6, 7, 5, 3, 1]
    return list(range(chips))


def tile_of(units):
    return 256 if units % 256 == 0 else units


def products(lefts, weights):
    total = None
    for i, weight in enumerate(weights):
        part = dot_t(lefts[i][...], weight[...])
        total = part if total is None else total + part
    return total


def load(blocks, lefts, sems):
    half = lefts.shape[1] // 2
    copies = []
    for i, (array, row) in enumerate(blocks):
        rows = pl.ds((i % 2) * half, half)
        source = array.at[pl.ds(row * half, half)]
        copies.append(pltpu.make_async_copy(source, lefts.at[i // 2, rows], sems.at[i]))
    for copy in copies:
        copy.start()
    for copy in copies:
        copy.wait()


def step_kernel(count, src_ref, *refs):
    blocks, weights = refs[:count], refs[count : 2 * count]
    out_ref, lefts, sems = refs[-3:]
    before_ref = refs[2 * count] if len(refs) == 2 * count + 4 else None
    step = pl.program_id(0)

    @pl.when(step == 0)
    def _():
        load([(block, i) for block in blocks for i in range(2)], lefts, sems)

    total = products(lefts, weights)
    out_ref[step] = total if before_ref is None else total + before_ref[step]


def near_kernel(*refs):
    blocks, weight_ref, before_ref, out_ref = refs[:4], refs[4], refs[5], refs[6]
    tiles, _, tile = out_ref.shape
    for i in range(tiles):
        cols = slice(i * tile, (i + 1) * tile)
        total = before_ref[i]
        for m, block in enumerate(blocks):
            total = total + dot_t(block[...], weight_ref[m, cols, :])
        out_ref[i] = total


def near_step(blocks, columns, before):
    ins = [in_vmem(x) for x in (*blocks, columns, before)]
    return pl.pallas_call(
        near_kernel,
        in_specs=[WHOLE] * len(ins),
        out_specs=WHOLE,
        out_shape=pltpu.VMEM(before.shape, F32),
        input_output_aliases={len(ins) - 1: 0},
        cost_estimate=SMALL,
        compiler_params=pltpu.CompilerParams(vmem_limit_bytes=VMEM_LIMIT),
    )(*ins)


def projected(ups, proj_ref):
    total, tile = None, ups.shape[2]
    for i in range(ups.shape[0]):
        part = dot_t(ups[i], proj_ref[:, i * tile : (i + 1) * tile])
        total = part if total is None else total + part
    return total


def in_hbm(x):
    return pltpu.with_memory_space_constraint(x, pltpu.HBM)


def in_vmem(x):
    return pltpu.with_memory_space_constraint(x, pltpu.VMEM)


ANYWHERE = pl.BlockSpec(memory_space=pl.ANY)
WHOLE = pl.BlockSpec(memory_space=pltpu.VMEM)


def step_parts(units, weight):
    tokens, depth = units[0][0].shape
    tile = tile_of(weight.shape[0])
    ins = [in_hbm(array) if place == 0 else array for array, place in units]
    ins += [in_hbm(weight)] * len(units)
    specs = [ANYWHERE] * len(units)
    specs += [pl.BlockSpec((tile, depth), lambda i, s, m=m: (i, s[m])) for _, m in units]
    scratch = [
        pltpu.VMEM((len(units), tokens, depth), BF16),
        pltpu.SemaphoreType.DMA((2 * len(units),)),
    ]
    return ins, specs, scratch, tile


def add_step(src, units, weight, before):
    ins, specs, scratch, tile = step_parts(units, weight)
    tokens, hidden = units[0][0].shape[0], weight.shape[0]
    aliases = {}
    if before is not None:
        ins.append(in_vmem(before))
        specs.append(WHOLE)
        aliases = {len(ins): 0}
    return pl.pallas_call(
        functools.partial(step_kernel, len(units)),
        grid_spec=pltpu.PrefetchScalarGridSpec(
            num_scalar_prefetch=1,
            grid=(hidden // tile,),
            in_specs=specs,
            out_specs=WHOLE,
            scratch_shapes=scratch,
        ),
        out_shape=pltpu.VMEM((hidden // tile, tokens, tile), F32),
        input_output_aliases=aliases,
        cost_estimate=SMALL,
        compiler_params=pltpu.CompilerParams(vmem_limit_bytes=VMEM_LIMIT),
    )(src, *ins)


def columns_kernel(places, src_ref, weight_ref, out_ref, sems):
    depth = out_ref.shape[2]
    copies = []
    for i, place in enumerate(places):
        start = pl.multiple_of(src_ref[place] * depth, depth)
        copies.append(
            pltpu.make_async_copy(weight_ref.at[:, pl.ds(start, depth)], out_ref.at[i], sems.at[i])
        )
    for copy in copies:
        copy.start()
    for copy in copies:
        copy.wait()


def columns_of(src, weight, depth, places):
    return pl.pallas_call(
        functools.partial(columns_kernel, places),
        grid_spec=pltpu.PrefetchScalarGridSpec(
            num_scalar_prefetch=1,
            grid=(),
            in_specs=[ANYWHERE],
            out_specs=WHOLE,
            scratch_shapes=[pltpu.SemaphoreType.DMA((len(places),))],
        ),
        out_shape=pltpu.VMEM((len(places), weight.shape[0], depth), BF16),
        cost_estimate=SMALL,
        compiler_params=pltpu.CompilerParams(vmem_limit_bytes=VMEM_LIMIT),
    )(src, in_hbm(weight))


def last_kernel(*refs):
    halves = refs[:4]
    weight_ref, silu_ref, proj_ref, before_ref, high_ref, low_ref, out_ref, ups = refs[4:]
    half, tile = halves[0].shape[0], ups.shape[2]
    for i in range(ups.shape[0]):
        cols = slice(i * tile, (i + 1) * tile)
        for h in range(2):
            rows = slice(h * half, (h + 1) * half)
            grad = before_ref[i, rows, :]
            for m in range(2):
                grad = grad + dot_t(halves[2 * h + m][...], weight_ref[m, cols, :])
            ups[i, rows, :] = (grad * silu_ref[i, rows, :]).astype(BF16)
    b_high, b_low = parts_of(projected(ups, proj_ref))
    kos = b_high.shape[1]
    sums = jnp.dot(
        high_ref[...], jnp.concatenate([b_high, b_low], axis=1), preferred_element_type=F32
    )
    rest = jnp.dot(low_ref[...], b_high, preferred_element_type=F32)
    out_ref[...] = spread(sums[:, :kos] + (sums[:, kos:] + rest), out_ref.shape[0])


def last_step(halves, columns, silu, proj_up, before, up, pairs):
    tiles, tokens, tile = silu.shape
    kos = proj_up.shape[0]
    ins = [in_vmem(x) for x in (*halves, columns, silu, proj_up, before, *up)]
    return pl.pallas_call(
        last_kernel,
        in_specs=[WHOLE] * len(ins),
        out_specs=WHOLE,
        out_shape=jax.ShapeDtypeStruct((pairs, up[0].shape[0] // pairs * kos), F32),
        scratch_shapes=[pltpu.VMEM((tiles, tokens, tile), BF16)],
        cost_estimate=SMALL,
        compiler_params=pltpu.CompilerParams(vmem_limit_bytes=VMEM_LIMIT),
    )(*ins)


def own_kernel(gate_ref, up_ref, down_ref, silu_ref, out_ref, hidden):
    step, tile = pl.program_id(0), gate_ref.shape[1]
    gate = gate_ref[...].astype(F32)
    silu = gate / (1.0 + jnp.exp(-gate))
    silu_ref[step] = silu
    hidden[step] = (silu * up_ref[...].astype(F32)).astype(BF16)

    @pl.when(step == hidden.shape[0] - 1)
    def _():
        total = None
        for i in range(hidden.shape[0]):
            part = dot_t(down_ref[:, i * tile : (i + 1) * tile], hidden[i])
            total = part if total is None else total + part
        out_ref[...] = total


def own_parts(gate, up, in_down):
    tokens, units = gate.shape
    tile, kis = tile_of(units), in_down.shape[0]
    tiles = pl.BlockSpec((tokens, tile), lambda i: (0, i))
    return pl.pallas_call(
        own_kernel,
        grid=(units // tile,),
        in_specs=[tiles, tiles, pl.BlockSpec((kis, units), lambda i: (0, 0))],
        out_specs=(WHOLE, pl.BlockSpec((kis, tokens), lambda i: (0, 0))),
        out_shape=(
            pltpu.VMEM((units // tile, tokens, tile), F32),
            jax.ShapeDtypeStruct((kis, tokens), F32),
        ),
        scratch_shapes=[pltpu.VMEM((units // tile, tokens, tile), BF16)],
        cost_estimate=SMALL,
        compiler_params=pltpu.CompilerParams(vmem_limit_bytes=VMEM_LIMIT),
    )(in_hbm(gate), in_hbm(up), in_down)


def turned(q, kos):
    asked, size = q.shape[0], q.shape[1] // 2
    kis = size // kos

    def kernel(q_ref, out_ref, rows):
        rows[...] = q_ref[...].astype(F32).T
        for j in range(kis):
            out_ref[j * kos : (j + 1) * kos, :] = rows[pl.ds(j, kos, stride=kis), :].astype(BF16)

    return pl.pallas_call(
        kernel,
        grid=(2,),
        in_specs=[pl.BlockSpec((asked, size), lambda i: (0, i))],
        out_specs=pl.BlockSpec((size, asked), lambda i: (i, 0)),
        out_shape=jax.ShapeDtypeStruct((2 * size, asked), BF16),
        scratch_shapes=[pltpu.VMEM((size, asked), F32)],
        cost_estimate=SMALL,
        compiler_params=pltpu.CompilerParams(vmem_limit_bytes=VMEM_LIMIT),
    )(in_hbm(q))


def score_kernel(down_ref, up_ref, q_ref, out_ref):
    pairs, size = down_ref.shape
    total = None
    for i, ref in enumerate((down_ref, up_ref)):
        both = jnp.concatenate(parts_of(ref[...]), axis=0)
        part = jnp.dot(both, q_ref[i * size : (i + 1) * size, :], preferred_element_type=F32)
        total = part if total is None else total + part
    out_ref[...] = total[:pairs] + total[pairs:]


def score(down, up, q):
    return pl.pallas_call(
        score_kernel,
        out_shape=jax.ShapeDtypeStruct((down.shape[0], q.shape[1]), F32),
        cost_estimate=SMALL,
        compiler_params=pltpu.CompilerParams(vmem_limit_bytes=VMEM_LIMIT),
    )(down, up, q)


def parts_of(x):
    high = x.astype(BF16)
    return high, (x - high.astype(F32)).astype(BF16)


def weighted(weight, a):
    return parts_of(jnp.concatenate([weight * a[j : j + 1, :] for j in range(a.shape[0])], axis=0))


def spread(sums, pairs):
    return jnp.concatenate([sums[r : r + pairs] for r in range(0, sums.shape[0], pairs)], axis=1)


def first_kernel(core_ref, acts_ref, grad_ref, in_up_ref, columns_ref, keep_ref, give_ref):
    first = core_ref[0] == 0
    a, b = dot_t(in_up_ref[...], acts_ref[...]), dot_t(columns_ref[...], grad_ref[...])
    half = a.shape[0] // 2
    for rows, x in ((slice(0, half), a), (slice(half, 2 * half), b)):
        keep_ref[rows, :] = jnp.where(first, x[:half], x[half:])
        give_ref[rows, :] = jnp.where(first, x[half:], x[:half])


def first_parts(core, acts, grad, in_up, columns):
    shape = jax.ShapeDtypeStruct((in_up.shape[0], acts.shape[0]), F32)
    whole = pl.BlockSpec(memory_space=pltpu.VMEM)
    return pl.pallas_call(
        first_kernel,
        in_specs=[pl.BlockSpec(memory_space=pltpu.SMEM)] + [whole] * 4,
        out_specs=(whole, whole),
        out_shape=(shape, shape),
        cost_estimate=SMALL,
        compiler_params=pltpu.CompilerParams(vmem_limit_bytes=VMEM_LIMIT),
    )(core, acts, grad, in_up, columns)


def pair_kernel(place_ref, weight_ref, mine_ref, across_ref, mine1_ref, across1_ref, a_ref, high_ref, low_ref, out_ref):
    first, near = place_ref[0] == 0, place_ref[1] == 0
    rows = []
    for mine, across in ((mine_ref, across_ref), (mine1_ref, across1_ref)):
        mine, across = mine[...], across[...].astype(F32)
        rows.append((jnp.where(near, mine, across), jnp.where(near, across, mine)))
    (a0, b0), (a1, b1) = rows
    a_up = jnp.concatenate([jnp.where(first, a0, a1), jnp.where(first, a1, a0)], axis=0)
    b_down = jnp.concatenate([jnp.where(first, b0, b1), jnp.where(first, b1, b0)], axis=0)
    weight = weight_ref[...]
    high_ref[...], low_ref[...] = weighted(weight, a_up)
    b_high, b_low = parts_of(b_down)
    high, low = weighted(weight, a_ref[...])
    sums = dot_t(high, b_high) + (dot_t(high, b_low) + dot_t(low, b_high))
    out_ref[...] = spread(sums, weight.shape[0])


def pair_parts(place, weight, quarters, a_down):
    pairs, tokens = weight.shape
    kis, kos = a_down.shape[0], 2 * quarters[0].shape[0]
    shape = pltpu.VMEM((pairs * kis, tokens), BF16)
    return pl.pallas_call(
        pair_kernel,
        in_specs=[pl.BlockSpec(memory_space=pltpu.SMEM)] + [WHOLE] * 6,
        out_specs=(WHOLE, WHOLE, WHOLE),
        out_shape=(shape, shape, jax.ShapeDtypeStruct((pairs, kis * kos), F32)),
        cost_estimate=SMALL,
        compiler_params=pltpu.CompilerParams(vmem_limit_bytes=VMEM_LIMIT),
    )(place, weight, *quarters, a_down)


def swap(value, bit, devices):
    return lax.ppermute(value, "tensor", [(i, i ^ bit) for i in range(devices)])


def per_device(
    devices,
    activations,
    gate_pre,
    up_pre,
    out_grad,
    down_weight,
    in_proj_down,
    out_proj_down,
    in_proj_up,
    out_proj_up,
    segments,
    labels,
    queries,
):
    tokens, depth = out_grad.shape
    me = lax.axis_index("tensor")
    chips = devices // 2
    ring = ring_of(chips)
    far = chips // 2
    place = {chip: i for i, chip in enumerate(ring)}

    table = np.zeros((devices, devices), np.int32)
    for device in range(devices):
        chip, core = divmod(device, 2)
        order = [chip]
        for step in range(1, far):
            order += [ring[(place[chip] - step) % chips], ring[(place[chip] + step) % chips]]
        order.append(ring[(place[chip] + far) % chips])
        table[device] = [2 * c + k for c in order for k in (core, 1 - core)]
    src = lax.dynamic_index_in_dim(jnp.asarray(table), me, 0, keepdims=False)

    ahead = [
        (2 * ring[i] + core, 2 * ring[(i + 1) % chips] + core) for i in range(chips) for core in (0, 1)
    ]
    back = [(b, a) for a, b in ahead]

    pin = lax.optimization_barrier
    kis, kos = in_proj_up.shape[0], out_proj_up.shape[0]
    seq_count = labels.shape[0]
    pairs, half = seq_count // 2, tokens // 2

    core = (me % 2)[None]

    def send(forward, backward):
        return lax.ppermute(forward, "tensor", ahead), lax.ppermute(backward, "tensor", back)

    f, b = send(out_grad, out_grad)
    other = swap(out_grad, 1, devices)
    own_columns = lax.dynamic_slice_in_dim(out_proj_down, me * depth, depth, axis=1)
    keep, give = first_parts(core, activations, out_grad, in_proj_up, own_columns)
    part = keep + swap(give, 1, devices)
    gate_pre, up_pre, part = pin((gate_pre, up_pre, part))
    silu_gate, a_down = own_parts(gate_pre, up_pre, in_proj_down)
    bits = [1 << i for i in reversed(range(2, devices.bit_length() - 1))]
    rounds = [[]] + [[int(bit) for bit in some] for some in np.array_split(bits, far - 2)]
    row = part.shape[0] // 2
    side = (me // 2) % 2
    give = lax.dynamic_slice_in_dim(part, (1 - side) * row, row, axis=0)
    part = lax.dynamic_slice_in_dim(part, side * row, row, axis=0)

    def ask(part, step):
        return [swap(part.astype(BF16), bit, devices) for bit in rounds[step]]

    def added(part, theirs):
        for more in theirs:
            part = part + more.astype(F32)
        return part

    theirs = [swap(give.astype(BF16), 2, devices)]
    seqs = jnp.arange(seq_count, dtype=jnp.int32)[:, None]
    signs = (2 * labels - 1).astype(F32)
    per_seq = jnp.where(segments[None, :] == seqs, signs[:, None], F32(0.0))
    pair_weight = per_seq.reshape(pairs, 2, tokens).sum(axis=1)

    f, b, theirs, a_down, pair_weight = pin((f, b, theirs, a_down, pair_weight))
    part = added(part, theirs)
    known, came = None, (f, b)
    units = [(out_grad, 0), (other, 1)]
    for step in range(1, far):
        if step < far - 1:
            f, b = send(f, b)
            theirs = ask(part, step)
        else:
            f, b = send(f[:half], b[half:])
        place = 4 * step - 2
        theirs_of = [swap(array, 1, devices) for array in came]
        units += [(array, place + 2 * i) for i, array in enumerate(came)]
        units += [(array, place + 2 * i + 1) for i, array in enumerate(theirs_of)]
        if step == far - 2:
            q_turned = turned(queries, kos)
            columns = [
                columns_of(src, down_weight, depth, places)
                for places in ([place + i for i in (4, 6, 5, 7)], [devices - 2, devices - 1])
            ]
            src, columns, q_turned = pin((src, columns, q_turned))
        if step == far - 1:
            near = [part, swap(part, 1, devices)]
            beyond = [swap(part.astype(BF16), bit, devices) for bit in (2, 3)]
            quarters = [near[0], beyond[0], near[1], beyond[1]]
            known = near_step([array for array, _ in units], columns[0], known)
        else:
            known = add_step(src, units, down_weight, known)
            units = []
            f, b, theirs, known = pin((f, b, theirs, known))
            part = added(part, theirs)
            came = (f, b)
    f, b, known = pin((f, b, known))
    halves = [x for block in (f, b) for x in (block, swap(block, 1, devices))]
    known, quarters = pin((known, quarters))
    high, low, down = pair_parts(jnp.stack([me % 2, side]), pair_weight, quarters, a_down)
    up = last_step(halves, columns[1], silu_gate, out_proj_up, known, (high, low), pairs)

    first = core == 0
    total = jnp.where(first, down, up) + swap(jnp.where(first, up, down), 1, devices)
    for bit in range(1, devices.bit_length() - 1):
        total = total + swap(total.astype(BF16), 1 << bit, devices).astype(F32)
    rest = swap(total, 1, devices)
    return score(jnp.where(first, total, rest), jnp.where(first, rest, total), q_turned)


def solution(mesh):
    in_specs = (
        P("groups", "tensor"),
        P("groups", "tensor"),
        P("groups", "tensor"),
        P("groups", "tensor"),
        P("tensor", None),
        P(None, "tensor"),
        P(),
        P(None, "tensor"),
        P(None, "tensor"),
        P("groups"),
        P("groups"),
        P("tensor", None),
    )
    return jax.shard_map(
        functools.partial(per_device, mesh.shape["tensor"]),
        mesh=mesh,
        in_specs=in_specs,
        out_specs=P("groups", "tensor"),
        check_vma=False,
    )
```
